32 devices in a mesh: tm: 32 (over z, y, x, core).
Axes of the slice: x: 2, y: 2, z: 4, core: 2. Of those that a mesh axis runs over, the one named last changes fastest.
Arguments:
- queries: bfloat16 [128, 32, 640], P('tm'), may hold values from -8 to 8
- keys: bfloat16 [128, 32, 640], P('tm'), may hold values from -8 to 8
- values: bfloat16 [128, 32, 640], P('tm'), may hold values from -8 to 8
- out_grad: bfloat16 [128, 32, 640], P('tm'), may hold values from -8 to 8
- clip_lengths: int32 [16], replicated, may hold values from 1 to 24, 128 in all
Outputs:
- attended: bfloat16 [128, 32, 640], P('tm')
- grad_queries: bfloat16 [128, 32, 640], P('tm')
- grad_keys: bfloat16 [128, 32, 640], P('tm')
- grad_values: bfloat16 [128, 32, 640], P('tm')
The draws below stay inside these ranges and needn't reach their ends.
Inputs may be any that keep to these rules, and one draw needn't show every extreme that they name: `clip_lengths`: lengths sum to 128; the longest clip has exactly 24 frames.
All inputs are finite; a program needn't handle non-finite values.
Results may differ from the reference program's by a relative error of at most 0.0088.
Values may be sent and summed in bfloat16 or wider, within the bound.
A program may use at most 64 MiB of HBM per device.

```python
import math
import jax
import jax.numpy as jnp
import numpy as np
from jax import lax

HEADS = 10
HEAD = 64
D = 640
TOK = 32
MAXCLIP = 24
FRAMES = 128
CLIPS = 16


def rough_base(key):
    return jax.random.truncated_normal(jax.random.fold_in(key, 5), -8.0, 8.0, (FRAMES, TOK, D), jnp.float32)


def draw_queries(key, part):
    own_key = jax.random.fold_in(key, 11)
    base = rough_base(own_key)
    return base.astype(jnp.bfloat16)


def draw_keys(key, part):
    own_key = jax.random.fold_in(key, 22)
    base = rough_base(own_key)
    return base.astype(jnp.bfloat16)


def steps_of(stream_key, shape, cuts, smallest, largest):
    factor_of, own = 1.0, jax.random.fold_in(stream_key, 6)
    for dim, parts in cuts:
        steps = jnp.exp(jax.random.uniform(jax.random.fold_in(own, dim), (parts,), jnp.float32, smallest / len(cuts), largest / len(cuts)))
        factor_of = factor_of * jnp.repeat(steps, shape[dim] // parts).reshape([-1 if axis == dim else 1 for axis in range(len(shape))])
    return factor_of


def length_profile(amount, total, limit, skew):
    portions = [(1 << 20) // math.isqrt(standing ** skew) + 1 for standing in range(2, amount + 1)]
    surplus, holding = total - limit - (amount - 1), [1] * (amount - 1)
    while surplus > 0:
        free = [i for i in range(amount - 1) if holding[i] < limit]
        pool, left = sum([portions[i] for i in free]), surplus
        for i in free:
            more = min(limit - holding[i], max(1, left * portions[i] // pool), surplus)
            holding[i] = holding[i] + more
            surplus = surplus - more
    return np.array([limit] + holding)


def uneven(rng, count, total, bound, lean):
    if count == 2:
        one = jax.random.randint(rng, (), max(1, total - bound), min(bound, total - 1) + 1)
        return jnp.stack([one, total - one])
    lengths = jnp.asarray(length_profile(count, total, bound, lean), jnp.int32)
    pairs = (count - 1) // 2
    donor, receiver = lengths[1:1 + 2 * pairs:2], lengths[2:2 + 2 * pairs:2]
    room = jnp.minimum(donor - 1, bound - receiver)
    shifted = jax.random.randint(jax.random.fold_in(rng, 1), (pairs,), 0, 1 << 20) % (room + 1)
    lengths = lengths.at[1:1 + 2 * pairs:2].set(donor - shifted).at[2:2 + 2 * pairs:2].set(receiver + shifted)
    return lengths[jax.random.permutation(jax.random.fold_in(rng, 2), count)]


def centred(key, dims, deviation, bound, split=(), kind=jnp.bfloat16):
    level = steps_of(key, dims, split, -0.22, 0.18) if split else 1.0
    result = jax.random.normal(key, dims, jnp.float32) * deviation * level
    return jnp.minimum(jnp.maximum(result, -bound), bound).astype(kind)


def setup_inputs(seed: int = 0) -> dict:
    arg_keys = jax.random.split(jax.random.key(seed), 6)
    queries = draw_queries(jax.random.fold_in(arg_keys[5], 71), 0)
    keys = draw_keys(jax.random.fold_in(arg_keys[5], 71), 0)
    values = centred(arg_keys[2], (FRAMES, TOK, D), 1.0, 8.0, ((0, 32),))
    out_grad = centred(arg_keys[3], (FRAMES, TOK, D), 1.0, 8.0, ((0, 32),))
    clip_lengths = uneven(arg_keys[4], CLIPS, FRAMES, MAXCLIP, 2).astype(jnp.int32)
    return dict(queries=queries, keys=keys, values=values, out_grad=out_grad, clip_lengths=clip_lengths)


def attend_frame(query, key_cat, value_cat, grad_out):
    score_scale = HEAD ** -0.5
    query_heads = query.astype(jnp.float32).reshape(TOK, HEADS, HEAD)
    key_heads = key_cat.astype(jnp.float32).reshape(2 * TOK, HEADS, HEAD)
    value_heads = value_cat.astype(jnp.float32).reshape(2 * TOK, HEADS, HEAD)
    grad_heads = grad_out.astype(jnp.float32).reshape(TOK, HEADS, HEAD)
    scores = jnp.einsum("qhd,khd->hqk", query_heads, key_heads) * score_scale
    row_max = jnp.max(scores, axis=-1, keepdims=True)
    expos = jnp.exp(scores - row_max)
    attn_prob = expos / jnp.sum(expos, axis=-1, keepdims=True)
    prob_low = lax.optimization_barrier(attn_prob.astype(jnp.bfloat16)).astype(jnp.float32)
    attended = jnp.einsum("hqk,khd->qhd", prob_low, value_heads).reshape(TOK, D).astype(jnp.bfloat16)
    grad_prob = jnp.einsum("qhd,khd->hqk", grad_heads, value_heads)
    grad_value = jnp.einsum("hqk,qhd->khd", prob_low, grad_heads).reshape(2 * TOK, D)
    grad_score = attn_prob * (grad_prob - jnp.sum(attn_prob * grad_prob, axis=-1, keepdims=True)) * score_scale
    score_low = lax.optimization_barrier(grad_score.astype(jnp.bfloat16)).astype(jnp.float32)
    grad_query = jnp.einsum("hqk,khd->qhd", score_low, key_heads).reshape(TOK, D).astype(jnp.bfloat16)
    grad_key = jnp.einsum("hqk,qhd->khd", score_low, query_heads).reshape(2 * TOK, D)
    return attended, grad_query, grad_key, grad_value


def reference(queries, keys, values, out_grad, clip_lengths):
    frame_ids = jnp.arange(FRAMES, dtype=jnp.int32)
    clip_ends = jnp.cumsum(clip_lengths).astype(jnp.int32)
    clip_starts = (clip_ends - clip_lengths).astype(jnp.int32)
    owner = jnp.max(jnp.where(clip_starts[None, :] <= frame_ids[:, None], clip_starts[None, :], 0), axis=1).astype(jnp.int32)
    previous = jnp.maximum(frame_ids - 1, owner).astype(jnp.int32)

    def advance(carry, inputs):
        acc_key, acc_value = carry
        query, grad_out, key_index, prev_index = inputs
        key_cat = jnp.concatenate([keys[key_index], keys[prev_index]], axis=0)
        value_cat = jnp.concatenate([values[key_index], values[prev_index]], axis=0)
        attended, grad_query, grad_key, grad_value = attend_frame(query, key_cat, value_cat, grad_out)
        acc_key = acc_key.at[key_index].add(grad_key[:TOK])
        acc_key = acc_key.at[prev_index].add(grad_key[TOK:])
        acc_value = acc_value.at[key_index].add(grad_value[:TOK])
        acc_value = acc_value.at[prev_index].add(grad_value[TOK:])
        return (acc_key, acc_value), (attended, grad_query)

    zeros = jnp.zeros((FRAMES, TOK, D), jnp.float32)
    (acc_key, acc_value), (attended, grad_query) = lax.scan(advance, (zeros, zeros), (queries, out_grad, owner, previous))
    return attended, grad_query, acc_key.astype(jnp.bfloat16), acc_value.astype(jnp.bfloat16)
```

```python
import functools

import jax
import jax.numpy as jnp
from jax import lax
from jax.experimental import pallas as pl
from jax.experimental.pallas import tpu as pltpu
from jax.sharding import PartitionSpec as P

HEADS = 10
MAXCLIP = 24
MESH = pl.DeviceIdType.MESH


def lane_groups(width, head):
    step = max(256, head)
    return [(start, min(step, width - start)) for start in range(0, width, step)]


def kernel(
    n, reach, groups, head,
    len_ref, q_ref, k_ref, v_ref, g_ref,
    att_ref, gq_ref, gk_ref, gv_ref,
    acc_k, acc_v, fsend, frecv, bsend, brecv, *bufs,
):
    count = len(groups)
    outs, pools = bufs[:count], bufs[count : 2 * count]
    gouts, gins = bufs[2 * count : 3 * count], bufs[3 * count : 4 * count]
    frames, tokens, _ = q_ref.shape
    me = lax.axis_index("tm")
    scale = head ** (-0.5)

    barrier = pltpu.get_barrier_semaphore()
    for k in range(1, reach + 1):
        @pl.when(me + k < n)
        def _():
            pl.semaphore_signal(barrier, inc=1, device_id=(me + k,), device_id_type=MESH)

        @pl.when(me >= k)
        def _():
            pl.semaphore_signal(barrier, inc=1, device_id=(me - k,), device_id_type=MESH)

    first = me * frames
    wanted = [first + f for f in range(frames)]
    wanted += [first + k * frames for k in range(1, reach + 1)]

    def scan_clips(c, carry):
        start, owners = carry
        owners = tuple(jnp.where(start <= w, start, o) for w, o in zip(wanted, owners))
        return start + len_ref[c], owners

    zero = jnp.int32(0)
    _, owners = lax.fori_loop(0, len_ref.shape[0], scan_clips, (zero, (zero,) * len(wanted)))
    local = [owners[f] - first for f in range(frames)]
    opening = [local[f] == f for f in range(frames)]
    has_start = local[frames - 1] >= 0
    last_open = jnp.clip(local[frames - 1], 0, frames - 1)
    back = jnp.clip(me - lax.div(owners[0], jnp.int32(frames)), 1, reach)
    owner_slot = [jnp.where(local[f] >= 0, local[f], frames + back) for f in range(frames)]
    prev_slot = [
        jnp.where(opening[f], f, f - 1 if f else frames) for f in range(frames)
    ]
    returns = []
    for k in range(1, reach + 1):
        owner = owners[frames + k - 1]
        mine = jnp.logical_and(owner >= first, owner < first + frames)
        returns.append(jnp.logical_and(mine, me + k < n))
    next_prev = jnp.logical_and(owners[frames] != first + frames, me + 1 < n)

    for i, (lo, w) in enumerate(groups):
        cols = slice(lo, lo + w)
        outs[i][0, 0] = k_ref[frames - 1, :, cols]
        outs[i][0, 1] = v_ref[frames - 1, :, cols]
        outs[i][1, 0] = k_ref[last_open, :, cols]
        outs[i][1, 1] = v_ref[last_open, :, cols]

    count_all = jnp.minimum(reach, n - 1 - me) + jnp.minimum(reach, me)
    pl.semaphore_wait(barrier, count_all)

    def forward(i, k):
        src = outs[i] if k == 1 else outs[i].at[1]
        dst = pools[i].at[pl.ds(frames, 2)] if k == 1 else pools[i].at[frames + k]
        return pltpu.make_async_remote_copy(
            src_ref=src, dst_ref=dst, send_sem=fsend.at[i, k - 1], recv_sem=frecv.at[i, k - 1],
            device_id=(jnp.minimum(me + k, n - 1),), device_id_type=MESH,
        )

    def backward(i, k):
        src = gouts[i] if k == 1 else gouts[i].at[1]
        dst = gins[i].at[pl.ds(0, 2)] if k == 1 else gins[i].at[k]
        return pltpu.make_async_remote_copy(
            src_ref=src, dst_ref=dst, send_sem=bsend.at[i, k - 1], recv_sem=brecv.at[i, k - 1],
            device_id=(jnp.maximum(me - k, 0),), device_id_type=MESH,
        )

    for i in range(count):
        for k in range(1, reach + 1):
            @pl.when(me + k < n)
            def _():
                forward(i, k).start()

    for i, (lo, w) in enumerate(groups):
        for f in range(frames):
            pools[i][f, 0] = k_ref[f, :, lo : lo + w]
            pools[i][f, 1] = v_ref[f, :, lo : lo + w]

    contract = lambda a, b, ca, cb: lax.dot_general(
        a, b, (((ca,), (cb,)), ((), ())), preferred_element_type=jnp.float32
    )

    for i, (lo, w) in enumerate(groups):
        cols = slice(lo, lo + w)
        heads = w // head
        lane = lax.broadcasted_iota(jnp.int32, (tokens, w), 1)
        inside = [jnp.logical_and(lane >= h * head, lane < (h + 1) * head) for h in range(heads)]
        keep = [m.astype(jnp.float32).astype(jnp.bfloat16) for m in inside]

        def stacked(x):
            return jnp.concatenate([x * keep[h] for h in range(heads)], axis=0)

        def unstacked(x):
            total = x[:tokens]
            for h in range(1, heads):
                total = jnp.where(inside[h], x[h * tokens : (h + 1) * tokens], total)
            return total

        for k in range(1, reach + 1):
            @pl.when(me >= k)
            def _():
                forward(i, k).wait_recv()

        sum_k, sum_v = [None] * frames, [None] * frames
        out_k = out_v = None

        def add(total, term):
            return term if total is None else total + term

        for f in range(frames):
            qs, gs = stacked(q_ref[f, :, cols]), stacked(g_ref[f, :, cols])
            own, prev = pools[i][owner_slot[f]], pools[i][prev_slot[f]]
            kcat = jnp.concatenate([own[0], prev[0]], axis=0)
            vcat = jnp.concatenate([own[1], prev[1]], axis=0)
            s = contract(kcat, qs, 1, 1) * scale
            dp = contract(vcat, gs, 1, 1)
            e = jnp.exp(s - jnp.max(s, axis=0, keepdims=True))
            p = e * (1.0 / jnp.sum(e, axis=0, keepdims=True))
            ds = p * (dp - jnp.sum(p * dp, axis=0, keepdims=True)) * scale
            p_low, ds_low = p.astype(jnp.bfloat16), ds.astype(jnp.bfloat16)
            att_ref[f, :, cols] = unstacked(contract(p_low, vcat, 0, 0)).astype(jnp.bfloat16)
            gq_ref[f, :, cols] = unstacked(contract(ds_low, kcat, 0, 0)).astype(jnp.bfloat16)
            dv = contract(p_low, gs, 1, 0)
            dk = contract(ds_low, qs, 1, 0)
            for t in range(f + 1):
                here = local[f] == t
                sum_k[t] = add(sum_k[t], jnp.where(here, dk[:tokens], 0.0))
                sum_v[t] = add(sum_v[t], jnp.where(here, dv[:tokens], 0.0))
            remote = local[f] < 0
            out_k = add(out_k, jnp.where(remote, dk[:tokens], 0.0))
            out_v = add(out_v, jnp.where(remote, dv[:tokens], 0.0))
            sum_k[f] = sum_k[f] + jnp.where(opening[f], dk[tokens:], 0.0)
            sum_v[f] = sum_v[f] + jnp.where(opening[f], dv[tokens:], 0.0)
            if f:
                sum_k[f - 1] = sum_k[f - 1] + jnp.where(opening[f], 0.0, dk[tokens:])
                sum_v[f - 1] = sum_v[f - 1] + jnp.where(opening[f], 0.0, dv[tokens:])
            else:
                gouts[i][0, 0] = dk[tokens:].astype(jnp.bfloat16)
                gouts[i][0, 1] = dv[tokens:].astype(jnp.bfloat16)
        gouts[i][1, 0] = out_k.astype(jnp.bfloat16)
        gouts[i][1, 1] = out_v.astype(jnp.bfloat16)
        for k in range(1, reach + 1):
            @pl.when(me >= k)
            def _():
                backward(i, k).start()
        for t in range(frames):
            acc_k[t, :, cols] = sum_k[t]
            acc_v[t, :, cols] = sum_v[t]

    for i, (lo, w) in enumerate(groups):
        cols = slice(lo, lo + w)
        for k in range(1, reach + 1):
            @pl.when(me + k < n)
            def _():
                backward(i, k).wait_recv()
        for part, (acc, result) in enumerate(((acc_k, gk_ref), (acc_v, gv_ref))):
            total = None
            for k in range(1, reach + 1):
                term = jnp.where(returns[k - 1], gins[i][k, part].astype(jnp.float32), 0.0)
                total = term if total is None else total + term
            for t in range(frames):
                value = acc[t, :, cols]
                here = jnp.logical_and(has_start, last_open == t)
                value = value + jnp.where(here, total, 0.0)
                if t == frames - 1:
                    edge = gins[i][0, part].astype(jnp.float32)
                    value = value + jnp.where(next_prev, edge, 0.0)
                result[t, :, cols] = value.astype(jnp.bfloat16)

    for i in range(count):
        for k in range(1, reach + 1):
            @pl.when(me + k < n)
            def _():
                forward(i, k).wait_send()

            @pl.when(me >= k)
            def _():
                backward(i, k).wait_send()


def body(n, queries, keys, values, out_grad, clip_lengths):
    frames, tokens, width = queries.shape
    head = width // HEADS
    reach = min(n - 1, -(-(MAXCLIP - 1) // frames))
    groups = lane_groups(width, head)
    half = jnp.bfloat16
    scratch = [pltpu.VMEM((frames, tokens, width), jnp.float32)] * 2
    scratch += [pltpu.SemaphoreType.DMA((len(groups), reach))] * 4
    scratch += [pltpu.VMEM((2, 2, tokens, w), half) for _, w in groups]
    scratch += [pltpu.VMEM((frames + 1 + reach, 2, tokens, w), half) for _, w in groups]
    scratch += [pltpu.VMEM((2, 2, tokens, w), half) for _, w in groups]
    scratch += [pltpu.VMEM((1 + reach, 2, tokens, w), half) for _, w in groups]
    vmem = pl.BlockSpec(memory_space=pltpu.VMEM)
    return pl.pallas_call(
        functools.partial(kernel, n, reach, groups, head),
        out_shape=[jax.ShapeDtypeStruct(queries.shape, half)] * 4,
        in_specs=[pl.BlockSpec(memory_space=pltpu.SMEM)] + [vmem] * 4,
        out_specs=[vmem] * 4,
        scratch_shapes=scratch,
        compiler_params=pltpu.CompilerParams(
            collective_id=0, has_side_effects=True, vmem_limit_bytes=48 * 1024 * 1024
        ),
    )(clip_lengths, queries, keys, values, out_grad)


def solution(mesh):
    split = P("tm", None, None)
    return jax.shard_map(
        functools.partial(body, mesh.shape["tm"]),
        mesh=mesh,
        in_specs=(split,) * 4 + (P(),),
        out_specs=(split,) * 4,
        check_vma=False,
    )
```

```python
import functools

import jax
import jax.numpy as jnp
from jax import lax
from jax.experimental import pallas as pl
from jax.experimental.pallas import tpu as pltpu
from jax.sharding import PartitionSpec as P

HEADS = 10
MAXCLIP = 24
MESH = pl.DeviceIdType.MESH


def lane_groups(width, head):
    step = max(256, head)
    return [(start, min(step, width - start)) for start in range(0, width, step)]


def kernel(
    n, reach, groups, head,
    len_ref, q_ref, k_ref, v_ref, g_ref,
    att_ref, gq_ref, gk_ref, gv_ref,
    lens, q_all, g_all, acc_k, acc_v, lsem, fsend, frecv, bsend, brecv, *bufs,
):
    count = len(groups)
    bufs = [bufs[j * count : (j + 1) * count] for j in range(len(bufs) // count)]
    starts, pools, chip_out, chip_in, qst, gst, gouts, gins, gchip_out, gchip_in, gtots = bufs
    frames, tokens, _ = q_ref.shape
    me = lax.axis_index("tm")
    core = lax.rem(me, 2)
    chip = lax.div(me, 2)
    chips = n // 2
    sibling = me + 1 - 2 * core
    scale = head ** (-0.5)
    edge, near, far = frames, frames + 1, frames + 2
    half = jnp.bfloat16

    loads = [pltpu.make_async_copy(len_ref, lens, lsem.at[0])]
    for i, (lo, w) in enumerate(groups):
        for part, ref in enumerate((k_ref, v_ref)):
            loads.append(pltpu.make_async_copy(
                ref.at[:, :, pl.ds(lo, w)], pools[i].at[pl.ds(0, frames), part],
                lsem.at[1 + 2 * i + part],
            ))
    late = [
        pltpu.make_async_copy(q_ref, q_all, lsem.at[1 + 2 * count]),
        pltpu.make_async_copy(g_ref, g_all, lsem.at[2 + 2 * count]),
    ]
    for copy in loads + late:
        copy.start()

    barrier = pltpu.get_barrier_semaphore()

    def greet(device):
        pl.semaphore_signal(barrier, inc=1, device_id=(device,), device_id_type=MESH)

    greet(sibling)
    for k in range(1, reach + 1):
        @pl.when(chip + k < chips)
        def _():
            greet(me + 2 * k)

        @pl.when(chip >= k)
        def _():
            greet(me - 2 * k)

    @pl.when(jnp.logical_and(core == 1, me + 1 < n))
    def _():
        greet(me + 1)

    @pl.when(jnp.logical_and(core == 0, me > 0))
    def _():
        greet(me - 1)

    greeted = 1 + jnp.minimum(reach, chips - 1 - chip) + jnp.minimum(reach, chip)
    greeted += jnp.where(core == 1, jnp.minimum(1, n - 1 - me), jnp.minimum(1, me))

    first = me * frames
    chip_first = chip * (2 * frames)
    wanted = [first + f for f in range(frames)]
    wanted += [chip_first, chip_first + frames, chip_first + 2 * frames - 1]
    wanted += [chip_first + k * 2 * frames for k in range(1, reach + 1)]
    loads[0].wait()

    def scan_clips(c, carry):
        start, owners = carry
        owners = tuple(jnp.where(start <= w, start, o) for w, o in zip(wanted, owners))
        return start + lens[c], owners

    zero = jnp.int32(0)
    _, owners = lax.fori_loop(0, len_ref.shape[0], scan_clips, (zero, (zero,) * len(wanted)))
    own_first, own_mid, own_last = owners[frames : frames + 3]
    own_later = owners[frames + 3 :]
    local = [owners[f] - first for f in range(frames)]
    opening = [local[f] == f for f in range(frames)]
    last_open = jnp.clip(local[frames - 1], 0, frames - 1)
    back = jnp.clip(chip - lax.div(own_first, jnp.int32(2 * frames)), 1, reach)
    away = [
        jnp.where(jnp.logical_and(core == 1, owners[f] >= chip_first), near, far)
        for f in range(frames)
    ]
    owner_slot = [jnp.where(local[f] >= 0, local[f], away[f]) for f in range(frames)]
    prev_slot = [jnp.where(opening[f], f, f - 1 if f else edge) for f in range(frames)]
    last_in_core1 = own_last >= chip_first + frames
    mid_outside = own_mid < chip_first
    mid_in_core0 = jnp.logical_and(
        core == 0, jnp.logical_and(own_mid >= chip_first, own_mid < chip_first + frames)
    )
    returns = [
        jnp.logical_and(
            chip + k < chips,
            jnp.logical_and(own_later[k - 1] >= chip_first, own_later[k - 1] < chip_first + 2 * frames),
        )
        for k in range(1, reach + 1)
    ]
    holder = jnp.logical_and(own_last >= first, own_last < first + frames)
    next_first = jnp.where(core == 0, own_mid, own_later[0])
    next_prev = jnp.logical_and(next_first != first + frames, me + 1 < n)

    def remote(src, dst, send, recv, i, slot, device):
        return pltpu.make_async_remote_copy(
            src_ref=src, dst_ref=dst, send_sem=send.at[i, slot], recv_sem=recv.at[i, slot],
            device_id=(device,), device_id_type=MESH,
        )

    after, before = jnp.minimum(me + 1, n - 1), jnp.maximum(me - 1, 0)
    fwd_edge = lambda i: remote(
        pools[i].at[frames - 1], pools[i].at[edge], fsend, frecv, i, 0, after)
    fwd_near0 = lambda i: remote(starts[i], pools[i].at[near], fsend, frecv, i, 1, sibling)
    fwd_near1 = lambda i: remote(
        starts[i].at[0], pools[i].at[near, 0], fsend, frecv, i, 1, sibling)
    fwd_far = lambda i: remote(
        pools[i].at[far, core], pools[i].at[far, core], fsend, frecv, i, 2, sibling)
    fwd_far_in = lambda i: remote(
        pools[i].at[far, core], pools[i].at[far, 1 - core], fsend, frecv, i, 2, sibling)
    fwd_chip = lambda i, k: remote(
        chip_out[i], chip_in[i].at[k - 1], fsend, frecv, i, 2 + k, jnp.minimum(me + 2 * k, n - 1))
    bwd_edge = lambda i: remote(gouts[i].at[0], gins[i].at[0], bsend, brecv, i, 0, before)
    bwd_near1 = lambda i: remote(gouts[i].at[1], gins[i].at[1], bsend, brecv, i, 1, sibling)
    bwd_near0 = lambda i: remote(
        gouts[i].at[1, 1], gins[i].at[1, 1], bsend, brecv, i, 1, sibling)
    bwd_tot = lambda i: remote(
        gtots[i].at[core], gtots[i].at[core], bsend, brecv, i, 2, sibling)
    bwd_tot_in = lambda i: remote(
        gtots[i].at[core], gtots[i].at[1 - core], bsend, brecv, i, 2, sibling)
    bwd_chip = lambda i, k: remote(
        gchip_out[i], gchip_in[i].at[k - 1], bsend, brecv, i, 2 + k, jnp.maximum(me - 2 * k, 0))

    def when(condition, act):
        @pl.when(condition)
        def _():
            act()

    for copy in loads[1:]:
        copy.wait()
    for i in range(count):
        start = pools[i][0]
        for f in range(1, frames):
            start = jnp.where(last_open == f, pools[i][f], start)
        starts[i][...] = start
    pl.semaphore_wait(barrier, greeted)

    for i in range(count):
        when(core == 0, lambda: fwd_near0(i).start())
        when(core == 1, lambda: fwd_near1(i).start())
    for i in range(count):
        when(me + 1 < n, lambda: fwd_edge(i).start())

    for i in range(count):
        when(core == 1, lambda: fwd_near0(i).wait_recv())
        when(core == 0, lambda: fwd_near1(i).wait_recv())
        own, other = starts[i][core], pools[i][near, core]
        take_own = jnp.where(core == 1, last_in_core1, jnp.logical_not(last_in_core1))
        chip_out[i][...] = jnp.where(take_own, own, other)
        for k in range(1, reach + 1):
            when(chip + k < chips, lambda: fwd_chip(i, k).start())

    for copy in late:
        copy.wait()

    def masks(w):
        lane = lax.broadcasted_iota(jnp.int32, (tokens, w), 1)
        return [
            jnp.logical_and(lane >= h * head, lane < (h + 1) * head) for h in range(w // head)
        ]

    for i, (lo, w) in enumerate(groups):
        keep = [m.astype(jnp.float32).astype(half) for m in masks(w)]
        for f in range(frames):
            for h, m in enumerate(keep):
                rows = slice(h * tokens, (h + 1) * tokens)
                qst[i][f, rows] = q_all[f, :, lo : lo + w] * m
                gst[i][f, rows] = g_all[f, :, lo : lo + w] * m

    def contract(a, b, ca, cb):
        return lax.dot_general(
            a, b, (((ca,), (cb,)), ((), ())), preferred_element_type=jnp.float32
        )

    def relay(i):
        for k in range(1, reach + 1):
            when(chip >= k, lambda: fwd_chip(i, k).wait_recv())
        pools[i][far, core] = chip_in[i][back - 1]
        fwd_far(i).start()

    def compute(i):
        lo, w = groups[i]
        cols = slice(lo, lo + w)
        inside = masks(w)

        def unstacked(x):
            total = x[:tokens]
            for h in range(1, w // head):
                total = jnp.where(inside[h], x[h * tokens : (h + 1) * tokens], total)
            return total.astype(half)

        each = range(frames)
        own = [pools[i][owner_slot[f]] for f in each]
        prev = [pools[i][prev_slot[f]] for f in each]
        kcat = [jnp.concatenate([own[f][0], prev[f][0]], axis=0) for f in each]
        vcat = [jnp.concatenate([own[f][1], prev[f][1]], axis=0) for f in each]
        s = [contract(kcat[f], qst[i][f], 1, 1) * scale for f in each]
        dp = [contract(vcat[f], gst[i][f], 1, 1) for f in each]
        e = [jnp.exp(s[f] - jnp.max(s[f], axis=0, keepdims=True)) for f in each]
        p = [e[f] * (1.0 / jnp.sum(e[f], axis=0, keepdims=True)) for f in each]
        p_low = [p[f].astype(half) for f in each]
        ds = [p[f] * (dp[f] - jnp.sum(p[f] * dp[f], axis=0, keepdims=True)) * scale for f in each]
        ds_low = [ds[f].astype(half) for f in each]
        dv = [contract(p_low[f], gst[i][f], 1, 0) for f in each]
        dk = [contract(ds_low[f], qst[i][f], 1, 0) for f in each]
        for part, (d, acc) in enumerate(((dk, acc_k), (dv, acc_v))):
            gouts[i][0, part] = d[0][tokens:].astype(half)
            out = jnp.zeros((tokens, w), jnp.float32)
            for f in each:
                out = out + jnp.where(local[f] < 0, d[f][:tokens], 0.0)
            gouts[i][1, part] = out.astype(half)
            for t in each:
                total = jnp.where(opening[t], d[t][tokens:], 0.0)
                if t + 1 < frames:
                    total = total + jnp.where(opening[t + 1], 0.0, d[t + 1][tokens:])
                for f in range(t, frames):
                    total = total + jnp.where(local[f] == t, d[f][:tokens], 0.0)
                acc[t, :, cols] = total
        when(core == 1, lambda: bwd_near1(i).start())
        when(core == 0, lambda: bwd_near0(i).start())
        when(me > 0, lambda: bwd_edge(i).start())
        for f in each:
            att_ref[f, :, cols] = unstacked(contract(p_low[f], vcat[f], 0, 0))
            gq_ref[f, :, cols] = unstacked(contract(ds_low[f], kcat[f], 0, 0))

    def chip_sum(i):
        when(core == 0, lambda: bwd_near1(i).wait_recv())
        when(core == 1, lambda: bwd_near0(i).wait_recv())
        mine = gouts[i][1, core].astype(jnp.float32)
        other = gins[i][1, core].astype(jnp.float32)
        keep_mine = jnp.logical_or(core == 0, mid_outside)
        keep_other = jnp.logical_or(core == 1, mid_outside)
        both = jnp.where(keep_mine, mine, 0.0) + jnp.where(keep_other, other, 0.0)
        gchip_out[i][...] = both.astype(half)
        for k in range(1, reach + 1):
            when(chip >= k, lambda: bwd_chip(i, k).start())

    def returned(i):
        for k in range(1, reach + 1):
            when(chip + k < chips, lambda: bwd_chip(i, k).wait_recv())
        total = None
        for k in range(1, reach + 1):
            term = jnp.where(returns[k - 1], gchip_in[i][k - 1].astype(jnp.float32), 0.0)
            total = term if total is None else total + term
        gtots[i][core] = total.astype(half)
        bwd_tot(i).start()

    def finish(i):
        lo, w = groups[i]
        cols = slice(lo, lo + w)
        when(me + 1 < n, lambda: bwd_edge(i).wait_recv())
        bwd_tot_in(i).wait_recv()
        for part, (acc, result) in enumerate(((acc_k, gk_ref), (acc_v, gv_ref))):
            total = jnp.where(holder, gtots[i][part].astype(jnp.float32), 0.0)
            total = total + jnp.where(mid_in_core0, gins[i][1, part].astype(jnp.float32), 0.0)
            for t in range(frames):
                value = acc[t, :, cols] + jnp.where(last_open == t, total, 0.0)
                if t == frames - 1:
                    behind = gins[i][0, part].astype(jnp.float32)
                    value = value + jnp.where(next_prev, behind, 0.0)
                result[t, :, cols] = value.astype(half)

    relay(0)
    for i in range(count):
        if i + 1 < count:
            relay(i + 1)
        fwd_far_in(i).wait_recv()
        when(me > 0, lambda: fwd_edge(i).wait_recv())
        compute(i)
        if i:
            chip_sum(i - 1)
    chip_sum(count - 1)
    for i in range(count):
        returned(i)
    for i in range(count):
        finish(i)

    for i in range(count):
        when(core == 0, lambda: fwd_near0(i).wait_send())
        when(core == 1, lambda: fwd_near1(i).wait_send())
        when(core == 0, lambda: bwd_near0(i).wait_send())
        when(core == 1, lambda: bwd_near1(i).wait_send())
        when(me + 1 < n, lambda: fwd_edge(i).wait_send())
        when(me > 0, lambda: bwd_edge(i).wait_send())
        fwd_far(i).wait_send()
        bwd_tot(i).wait_send()
        for k in range(1, reach + 1):
            when(chip + k < chips, lambda: fwd_chip(i, k).wait_send())
            when(chip >= k, lambda: bwd_chip(i, k).wait_send())


def store_kernel(*refs):
    count = len(refs) // 2
    sems = refs[-1]
    copies = [
        pltpu.make_async_copy(refs[j], refs[count + j], sems.at[j]) for j in range(count)
    ]
    for copy in copies:
        copy.start()
    for copy in copies:
        copy.wait()


def body(n, queries, keys, values, out_grad, clip_lengths):
    frames, tokens, width = queries.shape
    head = width // HEADS
    reach = min(n // 2 - 1, -(-(MAXCLIP - 1) // (2 * frames)))
    groups = lane_groups(width, head)
    count = len(groups)
    half = jnp.bfloat16
    scratch = [pltpu.SMEM(clip_lengths.shape, jnp.int32)]
    scratch += [pltpu.VMEM((frames, tokens, width), half)] * 2
    scratch += [pltpu.VMEM((frames, tokens, width), jnp.float32)] * 2
    scratch += [pltpu.SemaphoreType.DMA((3 + 2 * count,))]
    scratch += [pltpu.SemaphoreType.DMA((count, 3 + reach))] * 4
    shapes = [
        lambda w: (2, tokens, w),
        lambda w: (frames + 3, 2, tokens, w),
        lambda w: (tokens, w),
        lambda w: (reach, tokens, w),
        lambda w: (frames, w // head * tokens, w),
        lambda w: (frames, w // head * tokens, w),
        lambda w: (2, 2, tokens, w),
        lambda w: (2, 2, tokens, w),
        lambda w: (tokens, w),
        lambda w: (reach, tokens, w),
        lambda w: (2, tokens, w),
    ]
    scratch += [pltpu.VMEM(shape(w), half) for shape in shapes for _, w in groups]
    vmem = pl.BlockSpec(memory_space=pltpu.VMEM)
    hbm = pl.BlockSpec(memory_space=pltpu.HBM)
    like = [jax.ShapeDtypeStruct(queries.shape, half)] * 4
    args = (clip_lengths, queries, keys, values, out_grad)
    results = pl.pallas_call(
        functools.partial(kernel, n, reach, groups, head),
        out_shape=like,
        in_specs=[hbm] * 5,
        out_specs=[vmem] * 4,
        scratch_shapes=scratch,
        compiler_params=pltpu.CompilerParams(
            collective_id=0, has_side_effects=True, vmem_limit_bytes=48 * 1024 * 1024
        ),
    )(*[pltpu.with_memory_space_constraint(a, pltpu.HBM) for a in args])
    return pl.pallas_call(
        store_kernel,
        out_shape=like,
        in_specs=[vmem] * 4,
        out_specs=[hbm] * 4,
        scratch_shapes=[pltpu.SemaphoreType.DMA((4,))],
    )(*results)


def solution(mesh):
    split = P("tm", None, None)
    return jax.shard_map(
        functools.partial(body, mesh.shape["tm"]),
        mesh=mesh,
        in_specs=(split,) * 4 + (P(),),
        out_specs=(split,) * 4,
        check_vma=False,
    )
```

```python
import functools

import jax
import jax.numpy as jnp
from jax import lax
from jax.experimental import pallas as pl
from jax.experimental.pallas import tpu as pltpu
from jax.sharding import PartitionSpec as P

HEADS = 10
MAXCLIP = 24
MESH = pl.DeviceIdType.MESH


def lane_groups(width, head):
    step = max(256, head)
    return [(start, min(step, width - start)) for start in range(0, width, step)]


def kernel(
    n, reach, groups, head,
    len_ref, q_ref, k_ref, v_ref, g_ref,
    att_ref, gq_ref, gk_ref, gv_ref,
    lens, q_all, g_all, acc_k, acc_v, edges, gedge_out, gedge_in,
    lsem, esend, erecv, fsend, frecv, bsend, brecv, *bufs,
):
    count = len(groups)
    bufs = [bufs[j * count : (j + 1) * count] for j in range(len(bufs) // count)]
    starts, pools, chip_out, chip_in, qst, gst, pst, dst = bufs[:8]
    gouts, gins, gchip_out, gchip_in, gtots = bufs[8:]
    frames, tokens, _ = q_ref.shape
    me = lax.axis_index("tm")
    core = lax.rem(me, 2)
    chip = lax.div(me, 2)
    chips = n // 2
    sibling = me + 1 - 2 * core
    scale = head ** (-0.5)
    near, far = frames, frames + 1
    half = jnp.bfloat16

    loads = [pltpu.make_async_copy(len_ref, lens, lsem.at[0])]
    for i, (lo, w) in enumerate(groups):
        for part, ref in enumerate((k_ref, v_ref)):
            loads.append(pltpu.make_async_copy(
                ref.at[:, :, pl.ds(lo, w)], pools[i].at[pl.ds(0, frames), part],
                lsem.at[1 + 2 * i + part],
            ))
    late = [
        pltpu.make_async_copy(q_ref, q_all, lsem.at[1 + 2 * count]),
        pltpu.make_async_copy(g_ref, g_all, lsem.at[2 + 2 * count]),
    ]
    for copy in loads + late:
        copy.start()

    barrier = pltpu.get_barrier_semaphore()

    def greet(device):
        pl.semaphore_signal(barrier, inc=1, device_id=(device,), device_id_type=MESH)

    greet(sibling)
    for k in range(1, reach + 1):
        @pl.when(chip + k < chips)
        def _():
            greet(me + 2 * k)

        @pl.when(chip >= k)
        def _():
            greet(me - 2 * k)

    @pl.when(jnp.logical_and(core == 1, me + 1 < n))
    def _():
        greet(me + 1)

    @pl.when(jnp.logical_and(core == 0, me > 0))
    def _():
        greet(me - 1)

    greeted = 1 + jnp.minimum(reach, chips - 1 - chip) + jnp.minimum(reach, chip)
    greeted += jnp.where(core == 1, jnp.minimum(1, n - 1 - me), jnp.minimum(1, me))

    first = me * frames
    chip_first = chip * (2 * frames)
    wanted = [first + f for f in range(frames)]
    wanted += [chip_first, chip_first + frames, chip_first + 2 * frames - 1]
    wanted += [chip_first + k * 2 * frames for k in range(1, reach + 1)]
    loads[0].wait()

    def scan_clips(c, carry):
        start, owners = carry
        owners = tuple(jnp.where(start <= w, start, o) for w, o in zip(wanted, owners))
        return start + lens[c], owners

    zero = jnp.int32(0)
    _, owners = lax.fori_loop(0, len_ref.shape[0], scan_clips, (zero, (zero,) * len(wanted)))
    own_first, own_mid, own_last = owners[frames : frames + 3]
    own_later = owners[frames + 3 :]
    local = [owners[f] - first for f in range(frames)]
    opening = [local[f] == f for f in range(frames)]
    last_open = jnp.clip(local[frames - 1], 0, frames - 1)
    back = jnp.clip(chip - lax.div(own_first, jnp.int32(2 * frames)), 1, reach)
    away = [
        jnp.where(jnp.logical_and(core == 1, owners[f] >= chip_first), near, far)
        for f in range(frames)
    ]
    owner_slot = [jnp.where(local[f] >= 0, local[f], away[f]) for f in range(frames)]
    prev_slot = [jnp.where(opening[f], f, f - 1) for f in range(1, frames)]
    last_in_core1 = own_last >= chip_first + frames
    mid_outside = own_mid < chip_first
    mid_in_core0 = jnp.logical_and(
        core == 0, jnp.logical_and(own_mid >= chip_first, own_mid < chip_first + frames)
    )
    returns = [
        jnp.logical_and(
            chip + k < chips,
            jnp.logical_and(own_later[k - 1] >= chip_first, own_later[k - 1] < chip_first + 2 * frames),
        )
        for k in range(1, reach + 1)
    ]
    holder = jnp.logical_and(own_last >= first, own_last < first + frames)
    next_first = jnp.where(core == 0, own_mid, own_later[0])
    next_prev = jnp.logical_and(next_first != first + frames, me + 1 < n)

    def ends(src, dst, send_sem, recv_sem, device):
        return pltpu.make_async_remote_copy(
            src_ref=src, dst_ref=dst, send_sem=send_sem, recv_sem=recv_sem,
            device_id=(device,), device_id_type=MESH,
        )

    def remote(src, dst, send, recv, i, slot, device):
        return ends(src, dst, send.at[i, slot], recv.at[i, slot], device)

    after, before = jnp.minimum(me + 1, n - 1), jnp.maximum(me - 1, 0)
    fwd_edge = lambda part: ends(
        (k_ref, v_ref)[part].at[frames - 1], edges.at[part], esend.at[part], erecv.at[part], after)
    bwd_edge = lambda: ends(gedge_out, gedge_in, esend.at[2], erecv.at[2], before)
    fwd_near0 = lambda i: remote(starts[i], pools[i].at[near], fsend, frecv, i, 0, sibling)
    fwd_near1 = lambda i: remote(
        starts[i].at[0], pools[i].at[near, 0], fsend, frecv, i, 0, sibling)
    fwd_far = lambda i: remote(
        pools[i].at[far, core], pools[i].at[far, core], fsend, frecv, i, 1, sibling)
    fwd_far_in = lambda i: remote(
        pools[i].at[far, core], pools[i].at[far, 1 - core], fsend, frecv, i, 1, sibling)
    fwd_chip = lambda i, k: remote(
        chip_out[i], chip_in[i].at[k - 1], fsend, frecv, i, 1 + k, jnp.minimum(me + 2 * k, n - 1))
    bwd_near1 = lambda i: remote(gouts[i], gins[i], bsend, brecv, i, 0, sibling)
    bwd_near0 = lambda i: remote(gouts[i].at[1], gins[i].at[1], bsend, brecv, i, 0, sibling)
    bwd_tot = lambda i: remote(
        gtots[i].at[core], gtots[i].at[core], bsend, brecv, i, 1, sibling)
    bwd_tot_in = lambda i: remote(
        gtots[i].at[core], gtots[i].at[1 - core], bsend, brecv, i, 1, sibling)
    bwd_chip = lambda i, k: remote(
        gchip_out[i], gchip_in[i].at[k - 1], bsend, brecv, i, 1 + k, jnp.maximum(me - 2 * k, 0))

    def when(condition, act):
        @pl.when(condition)
        def _():
            act()

    for copy in loads[1:]:
        copy.wait()
    for i in range(count):
        start = pools[i][0]
        for f in range(1, frames):
            start = jnp.where(last_open == f, pools[i][f], start)
        starts[i][...] = start
    pl.semaphore_wait(barrier, greeted)

    for i in range(count):
        when(core == 0, lambda: fwd_near0(i).start())
        when(core == 1, lambda: fwd_near1(i).start())
    for part in range(2):
        when(me + 1 < n, lambda: fwd_edge(part).start())

    for i in range(count):
        when(core == 1, lambda: fwd_near0(i).wait_recv())
        when(core == 0, lambda: fwd_near1(i).wait_recv())
        own, other = starts[i][core], pools[i][near, core]
        take_own = jnp.where(core == 1, last_in_core1, jnp.logical_not(last_in_core1))
        chip_out[i][...] = jnp.where(take_own, own, other)
        for k in range(1, reach + 1):
            when(chip + k < chips, lambda: fwd_chip(i, k).start())

    for copy in late:
        copy.wait()

    def masks(w):
        lane = lax.broadcasted_iota(jnp.int32, (tokens, w), 1)
        return [
            jnp.logical_and(lane >= h * head, lane < (h + 1) * head) for h in range(w // head)
        ]

    for i, (lo, w) in enumerate(groups):
        keep = [m.astype(jnp.float32).astype(half) for m in masks(w)]
        for f in range(frames):
            for h, m in enumerate(keep):
                rows = slice(h * tokens, (h + 1) * tokens)
                qst[i][f, rows] = q_all[f, :, lo : lo + w] * m
                gst[i][f, rows] = g_all[f, :, lo : lo + w] * m

    def contract(a, b, ca, cb):
        return lax.dot_general(
            a, b, (((ca,), (cb,)), ((), ())), preferred_element_type=jnp.float32
        )

    def relay(i):
        for k in range(1, reach + 1):
            when(chip >= k, lambda: fwd_chip(i, k).wait_recv())
        pools[i][far, core] = chip_in[i][back - 1]
        fwd_far(i).start()

    each = range(frames)

    def frame_sets(i):
        lo, w = groups[i]
        own = [pools[i][owner_slot[f]] for f in each]
        prev = [jnp.where(opening[0], pools[i][0], edges[:, :, lo : lo + w])]
        prev += [pools[i][prev_slot[f - 1]] for f in each[1:]]
        return [
            [jnp.concatenate([own[f][part], prev[f][part]], axis=0) for f in each]
            for part in range(2)
        ]

    def scores(i):
        kcat, vcat = frame_sets(i)
        s = [contract(kcat[f], qst[i][f], 1, 1) * scale for f in each]
        dp = [contract(vcat[f], gst[i][f], 1, 1) for f in each]
        e = [jnp.exp(s[f] - jnp.max(s[f], axis=0, keepdims=True)) for f in each]
        p = [e[f] * (1.0 / jnp.sum(e[f], axis=0, keepdims=True)) for f in each]
        ds = [p[f] * (dp[f] - jnp.sum(p[f] * dp[f], axis=0, keepdims=True)) * scale for f in each]
        for f in each:
            pst[i][f] = p[f].astype(half)
            dst[i][f] = ds[f].astype(half)

    def key_grads(i):
        lo, w = groups[i]
        cols = slice(lo, lo + w)
        dk = [contract(dst[i][f], qst[i][f], 1, 0) for f in each]
        dv = [contract(pst[i][f], gst[i][f], 1, 0) for f in each]
        for part, d in enumerate((dk, dv)):
            gedge_out[part, :, cols] = d[0][tokens:].astype(half)
            out = jnp.zeros((tokens, w), jnp.float32)
            for f in each:
                out = out + jnp.where(local[f] < 0, d[f][:tokens], 0.0)
            gouts[i][part] = out.astype(half)
        when(core == 1, lambda: bwd_near1(i).start())
        when(core == 0, lambda: bwd_near0(i).start())
        for d, acc in ((dk, acc_k), (dv, acc_v)):
            for t in each:
                total = jnp.where(opening[t], d[t][tokens:], 0.0)
                if t + 1 < frames:
                    total = total + jnp.where(opening[t + 1], 0.0, d[t + 1][tokens:])
                for f in range(t, frames):
                    total = total + jnp.where(local[f] == t, d[f][:tokens], 0.0)
                acc[t, :, cols] = total

    def frame_outputs(i):
        lo, w = groups[i]
        cols = slice(lo, lo + w)
        inside = masks(w)

        def unstacked(x):
            total = x[:tokens]
            for h in range(1, w // head):
                total = jnp.where(inside[h], x[h * tokens : (h + 1) * tokens], total)
            return total.astype(half)

        kcat, vcat = frame_sets(i)
        att = [contract(pst[i][f], vcat[f], 0, 0) for f in each]
        gq = [contract(dst[i][f], kcat[f], 0, 0) for f in each]
        for f in each:
            att_ref[f, :, cols] = unstacked(att[f])
            gq_ref[f, :, cols] = unstacked(gq[f])

    def chip_sum(i):
        when(core == 0, lambda: bwd_near1(i).wait_recv())
        when(core == 1, lambda: bwd_near0(i).wait_recv())
        mine = gouts[i][core].astype(jnp.float32)
        other = gins[i][core].astype(jnp.float32)
        keep_mine = jnp.logical_or(core == 0, mid_outside)
        keep_other = jnp.logical_or(core == 1, mid_outside)
        both = jnp.where(keep_mine, mine, 0.0) + jnp.where(keep_other, other, 0.0)
        gchip_out[i][...] = both.astype(half)
        for k in range(1, reach + 1):
            when(chip >= k, lambda: bwd_chip(i, k).start())

    def returned(i):
        for k in range(1, reach + 1):
            when(chip + k < chips, lambda: bwd_chip(i, k).wait_recv())
        total = None
        for k in range(1, reach + 1):
            term = jnp.where(returns[k - 1], gchip_in[i][k - 1].astype(jnp.float32), 0.0)
            total = term if total is None else total + term
        gtots[i][core] = total.astype(half)
        bwd_tot(i).start()

    def finish(i):
        lo, w = groups[i]
        cols = slice(lo, lo + w)
        bwd_tot_in(i).wait_recv()
        for part, (acc, result) in enumerate(((acc_k, gk_ref), (acc_v, gv_ref))):
            total = jnp.where(holder, gtots[i][part].astype(jnp.float32), 0.0)
            total = total + jnp.where(mid_in_core0, gins[i][part].astype(jnp.float32), 0.0)
            for t in range(frames):
                value = acc[t, :, cols] + jnp.where(last_open == t, total, 0.0)
                if t == frames - 1:
                    behind = gedge_in[part, :, cols].astype(jnp.float32)
                    value = value + jnp.where(next_prev, behind, 0.0)
                result[t, :, cols] = value.astype(half)

    relay(0)
    for i in range(count):
        fwd_far_in(i).wait_recv()
        if i == 0:
            for part in range(2):
                when(me > 0, lambda: fwd_edge(part).wait_recv())
        scores(i)
        if i + 1 < count:
            relay(i + 1)
        key_grads(i)
        if i:
            chip_sum(i - 1)
    when(me > 0, lambda: bwd_edge().start())
    frame_outputs(0)
    chip_sum(count - 1)
    for i in range(1, count):
        frame_outputs(i)
    for i in range(count):
        returned(i)
    when(me + 1 < n, lambda: bwd_edge().wait_recv())
    for i in range(count):
        finish(i)

    when(me > 0, lambda: bwd_edge().wait_send())
    for part in range(2):
        when(me + 1 < n, lambda: fwd_edge(part).wait_send())
    for i in range(count):
        when(core == 0, lambda: fwd_near0(i).wait_send())
        when(core == 1, lambda: fwd_near1(i).wait_send())
        when(core == 0, lambda: bwd_near0(i).wait_send())
        when(core == 1, lambda: bwd_near1(i).wait_send())
        fwd_far(i).wait_send()
        bwd_tot(i).wait_send()
        for k in range(1, reach + 1):
            when(chip + k < chips, lambda: fwd_chip(i, k).wait_send())
            when(chip >= k, lambda: bwd_chip(i, k).wait_send())


def store_kernel(*refs):
    count = len(refs) // 2
    sems = refs[-1]
    copies = [
        pltpu.make_async_copy(refs[j], refs[count + j], sems.at[j]) for j in range(count)
    ]
    for copy in copies:
        copy.start()
    for copy in copies:
        copy.wait()


def body(n, queries, keys, values, out_grad, clip_lengths):
    frames, tokens, width = queries.shape
    head = width // HEADS
    reach = min(n // 2 - 1, -(-(MAXCLIP - 1) // (2 * frames)))
    groups = lane_groups(width, head)
    count = len(groups)
    half = jnp.bfloat16
    scratch = [pltpu.SMEM(clip_lengths.shape, jnp.int32)]
    scratch += [pltpu.VMEM((frames, tokens, width), half)] * 2
    scratch += [pltpu.VMEM((frames, tokens, width), jnp.float32)] * 2
    scratch += [pltpu.VMEM((2, tokens, width), half)] * 3
    scratch += [pltpu.SemaphoreType.DMA((3 + 2 * count,))]
    scratch += [pltpu.SemaphoreType.DMA((3,))] * 2
    scratch += [pltpu.SemaphoreType.DMA((count, 2 + reach))] * 4
    shapes = [
        lambda w: (2, tokens, w),
        lambda w: (frames + 2, 2, tokens, w),
        lambda w: (tokens, w),
        lambda w: (reach, tokens, w),
        lambda w: (frames, w // head * tokens, w),
        lambda w: (frames, w // head * tokens, w),
        lambda w: (frames, 2 * tokens, w // head * tokens),
        lambda w: (frames, 2 * tokens, w // head * tokens),
        lambda w: (2, tokens, w),
        lambda w: (2, tokens, w),
        lambda w: (tokens, w),
        lambda w: (reach, tokens, w),
        lambda w: (2, tokens, w),
    ]
    scratch += [pltpu.VMEM(shape(w), half) for shape in shapes for _, w in groups]
    vmem = pl.BlockSpec(memory_space=pltpu.VMEM)
    hbm = pl.BlockSpec(memory_space=pltpu.HBM)
    like = [jax.ShapeDtypeStruct(queries.shape, half)] * 4
    args = (clip_lengths, queries, keys, values, out_grad)
    results = pl.pallas_call(
        functools.partial(kernel, n, reach, groups, head),
        out_shape=like,
        in_specs=[hbm] * 5,
        out_specs=[vmem] * 4,
        scratch_shapes=scratch,
        compiler_params=pltpu.CompilerParams(
            collective_id=0, has_side_effects=True, vmem_limit_bytes=48 * 1024 * 1024
        ),
    )(*[pltpu.with_memory_space_constraint(a, pltpu.HBM) for a in args])
    return pl.pallas_call(
        store_kernel,
        out_shape=like,
        in_specs=[vmem] * 4,
        out_specs=[hbm] * 4,
        scratch_shapes=[pltpu.SemaphoreType.DMA((4,))],
        compiler_params=pltpu.CompilerParams(vmem_limit_bytes=4 * 1024 * 1024),
    )(*[pltpu.with_memory_space_constraint(a, pltpu.VMEM) for a in results])


def solution(mesh):
    split = P("tm", None, None)
    return jax.shard_map(
        functools.partial(body, mesh.shape["tm"]),
        mesh=mesh,
        in_specs=(split,) * 4 + (P(),),
        out_specs=(split,) * 4,
        check_vma=False,
    )
```

```python
import functools

import jax
import jax.numpy as jnp
from jax import lax
from jax.experimental import pallas as pl
from jax.experimental.pallas import tpu as pltpu
from jax.sharding import PartitionSpec as P

HEADS = 10
MAXCLIP = 24
MESH = pl.DeviceIdType.MESH


def lane_groups(width, head):
    step = max(256, head)
    return [(start, min(step, width - start)) for start in range(0, width, step)]


def kernel(
    n, reach, groups, head,
    len_ref, q_ref, k_ref, v_ref, g_ref,
    att_ref, gq_ref, gk_ref, gv_ref,
    lens, q_all, g_all, acc_k, acc_v, lsem, fsend, frecv, bsend, brecv, *bufs,
):
    count = len(groups)
    bufs = [bufs[j * count : (j + 1) * count] for j in range(len(bufs) // count)]
    starts, pools, chip_out, chip_in, qst, gst, pst, dst = bufs[:8]
    gouts, gins, gchip_out, gchip_in, gtots, edges, gedge_out, gedge_in = bufs[8:]
    frames, tokens, _ = q_ref.shape
    me = lax.axis_index("tm")
    core = lax.rem(me, 2)
    chip = lax.div(me, 2)
    chips = n // 2
    sibling = me + 1 - 2 * core
    scale = head ** (-0.5)
    near, far = frames, frames + 1
    half = jnp.bfloat16

    loads = [pltpu.make_async_copy(len_ref, lens, lsem.at[0])]
    for i, (lo, w) in enumerate(groups):
        for part, ref in enumerate((k_ref, v_ref)):
            loads.append(pltpu.make_async_copy(
                ref.at[:, :, pl.ds(lo, w)], pools[i].at[pl.ds(0, frames), part],
                lsem.at[1 + 2 * i + part],
            ))
    late = [
        pltpu.make_async_copy(q_ref, q_all, lsem.at[1 + 2 * count]),
        pltpu.make_async_copy(g_ref, g_all, lsem.at[2 + 2 * count]),
    ]
    for copy in loads + late:
        copy.start()

    barrier = pltpu.get_barrier_semaphore()

    def greet(device):
        pl.semaphore_signal(barrier, inc=1, device_id=(device,), device_id_type=MESH)

    greet(sibling)
    for k in range(1, reach + 1):
        @pl.when(chip + k < chips)
        def _():
            greet(me + 2 * k)
            greet(sibling + 2 * k)

        @pl.when(chip >= k)
        def _():
            greet(me - 2 * k)
            greet(sibling - 2 * k)

    greeted = 1 + 2 * (jnp.minimum(reach, chips - 1 - chip) + jnp.minimum(reach, chip))

    first = me * frames
    chip_first = chip * (2 * frames)
    wanted = [first + f for f in range(frames)]
    wanted += [chip_first, chip_first + frames, chip_first + 2 * frames - 1]
    wanted += [chip_first + k * 2 * frames for k in range(1, reach + 1)]
    loads[0].wait()

    def scan_clips(c, carry):
        start, owners = carry
        owners = tuple(jnp.where(start <= w, start, o) for w, o in zip(wanted, owners))
        return start + lens[c], owners

    zero = jnp.int32(0)
    _, owners = lax.fori_loop(0, len_ref.shape[0], scan_clips, (zero, (zero,) * len(wanted)))
    own_first, own_mid, own_last = owners[frames : frames + 3]
    own_later = owners[frames + 3 :]
    local = [owners[f] - first for f in range(frames)]
    opening = [local[f] == f for f in range(frames)]
    last_open = jnp.clip(local[frames - 1], 0, frames - 1)
    back = jnp.clip(chip - lax.div(own_first, jnp.int32(2 * frames)), 1, reach)
    away = [
        jnp.where(jnp.logical_and(core == 1, owners[f] >= chip_first), near, far)
        for f in range(frames)
    ]
    owner_slot = [jnp.where(local[f] >= 0, local[f], away[f]) for f in range(frames)]
    prev_slot = [jnp.where(opening[f], f, f - 1) for f in range(1, frames)]
    last_in_core1 = own_last >= chip_first + frames
    mid_outside = own_mid < chip_first
    mid_in_core0 = jnp.logical_and(
        core == 0, jnp.logical_and(own_mid >= chip_first, own_mid < chip_first + frames)
    )
    returns = [
        jnp.logical_and(
            chip + k < chips,
            jnp.logical_and(own_later[k - 1] >= chip_first, own_later[k - 1] < chip_first + 2 * frames),
        )
        for k in range(1, reach + 1)
    ]
    holder = jnp.logical_and(own_last >= first, own_last < first + frames)
    next_first = jnp.where(core == 0, own_mid, own_later[0])
    next_prev = jnp.logical_and(next_first != first + frames, me + 1 < n)

    def ends(src, dst, send_sem, recv_sem, device):
        return pltpu.make_async_remote_copy(
            src_ref=src, dst_ref=dst, send_sem=send_sem, recv_sem=recv_sem,
            device_id=(device,), device_id_type=MESH,
        )

    def remote(src, dst, send, recv, i, slot, device):
        return ends(src, dst, send.at[i, slot], recv.at[i, slot], device)

    after, before = jnp.minimum(me + 1, n - 1), jnp.maximum(me - 1, 0)
    fwd_edge = lambda i: remote(
        pools[i].at[frames - 1], edges[i], fsend, frecv, i, 2 + reach, after)
    bwd_edge = lambda i: remote(gedge_out[i], gedge_in[i], bsend, brecv, i, 2 + reach, before)
    fwd_near0 = lambda i: remote(starts[i], pools[i].at[near], fsend, frecv, i, 0, sibling)
    fwd_near1 = lambda i: remote(
        starts[i].at[0], pools[i].at[near, 0], fsend, frecv, i, 0, sibling)
    fwd_far = lambda i: remote(
        pools[i].at[far, core], pools[i].at[far, core], fsend, frecv, i, 1, sibling)
    fwd_far_in = lambda i: remote(
        pools[i].at[far, core], pools[i].at[far, 1 - core], fsend, frecv, i, 1, sibling)
    fwd_chip = lambda i, k: remote(
        chip_out[i], chip_in[i].at[k - 1], fsend, frecv, i, 1 + k, jnp.minimum(me + 2 * k, n - 1))
    bwd_near1 = lambda i: remote(gouts[i], gins[i], bsend, brecv, i, 0, sibling)
    bwd_near0 = lambda i: remote(gouts[i].at[1], gins[i].at[1], bsend, brecv, i, 0, sibling)
    bwd_tot = lambda i: remote(
        gtots[i].at[core], gtots[i].at[core], bsend, brecv, i, 1, sibling)
    bwd_tot_in = lambda i: remote(
        gtots[i].at[core], gtots[i].at[1 - core], bsend, brecv, i, 1, sibling)
    bwd_chip = lambda i, k: remote(
        gchip_out[i], gchip_in[i].at[core, k - 1], bsend, brecv, i, 1 + k,
        jnp.maximum(me - 2 * k, 0))
    bwd_cross = lambda i, k: remote(
        gchip_out[i], gchip_in[i].at[core, k - 1], bsend, brecv, i, 2 + reach + k,
        jnp.maximum(sibling - 2 * k, 0))
    bwd_cross_in = lambda i, k: remote(
        gchip_out[i], gchip_in[i].at[1 - core, k - 1], bsend, brecv, i, 2 + reach + k,
        jnp.maximum(sibling - 2 * k, 0))

    def when(condition, act):
        @pl.when(condition)
        def _():
            act()

    for copy in loads[1:]:
        copy.wait()
    for i in range(count):
        start = pools[i][0]
        for f in range(1, frames):
            start = jnp.where(last_open == f, pools[i][f], start)
        starts[i][...] = start
    pl.semaphore_wait(barrier, greeted)

    for i in range(count):
        when(core == 0, lambda: fwd_near0(i).start())
        when(core == 1, lambda: fwd_near1(i).start())
    when(me + 1 < n, lambda: fwd_edge(0).start())

    for i in range(count):
        when(core == 1, lambda: fwd_near0(i).wait_recv())
        when(core == 0, lambda: fwd_near1(i).wait_recv())
        own, other = starts[i][core], pools[i][near, core]
        take_own = jnp.where(core == 1, last_in_core1, jnp.logical_not(last_in_core1))
        chip_out[i][...] = jnp.where(take_own, own, other)
        for k in range(1, reach + 1):
            when(chip + k < chips, lambda: fwd_chip(i, k).start())
        if i + 1 < count:
            when(me + 1 < n, lambda: fwd_edge(i + 1).start())

    for copy in late:
        copy.wait()

    def masks(w):
        lane = lax.broadcasted_iota(jnp.int32, (tokens, w), 1)
        return [
            jnp.logical_and(lane >= h * head, lane < (h + 1) * head) for h in range(w // head)
        ]

    for i, (lo, w) in enumerate(groups):
        keep = [m.astype(jnp.float32).astype(half) for m in masks(w)]
        for f in range(frames):
            for h, m in enumerate(keep):
                rows = slice(h * tokens, (h + 1) * tokens)
                qst[i][f, rows] = q_all[f, :, lo : lo + w] * m
                gst[i][f, rows] = g_all[f, :, lo : lo + w] * m

    def contract(a, b, ca, cb):
        return lax.dot_general(
            a, b, (((ca,), (cb,)), ((), ())), preferred_element_type=jnp.float32
        )

    def relay(i):
        for k in range(1, reach + 1):
            when(chip >= k, lambda: fwd_chip(i, k).wait_recv())
        pools[i][far, core] = chip_in[i][back - 1]
        fwd_far(i).start()

    each = range(frames)

    def frame_sets(i):
        own = [pools[i][owner_slot[f]] for f in each]
        prev = [jnp.where(opening[0], pools[i][0], edges[i][...])]
        prev += [pools[i][prev_slot[f - 1]] for f in each[1:]]
        return [
            [jnp.concatenate([own[f][part], prev[f][part]], axis=0) for f in each]
            for part in range(2)
        ]

    def scores(i):
        kcat, vcat = frame_sets(i)
        s = [contract(kcat[f], qst[i][f], 1, 1) * scale for f in each]
        dp = [contract(vcat[f], gst[i][f], 1, 1) for f in each]
        if i:
            frame_outputs(i - 1)
        e = [jnp.exp(s[f] - jnp.max(s[f], axis=0, keepdims=True)) for f in each]
        p = [e[f] * (1.0 / jnp.sum(e[f], axis=0, keepdims=True)) for f in each]
        ds = [p[f] * (dp[f] - jnp.sum(p[f] * dp[f], axis=0, keepdims=True)) * scale for f in each]
        for f in each:
            pst[i][f] = p[f].astype(half)
            dst[i][f] = ds[f].astype(half)

    def key_grads(i):
        lo, w = groups[i]
        cols = slice(lo, lo + w)
        dk = [contract(dst[i][f], qst[i][f], 1, 0) for f in each]
        dv = [contract(pst[i][f], gst[i][f], 1, 0) for f in each]
        for part, d in enumerate((dk, dv)):
            gedge_out[i][part] = d[0][tokens:].astype(half)
            out = jnp.zeros((tokens, w), jnp.float32)
            for f in each:
                out = out + jnp.where(local[f] < 0, d[f][:tokens], 0.0)
            gouts[i][part] = out.astype(half)
        when(core == 1, lambda: bwd_near1(i).start())
        when(core == 0, lambda: bwd_near0(i).start())
        when(me > 0, lambda: bwd_edge(i).start())
        for d, acc in ((dk, acc_k), (dv, acc_v)):
            for t in each:
                total = jnp.where(opening[t], d[t][tokens:], 0.0)
                if t + 1 < frames:
                    total = total + jnp.where(opening[t + 1], 0.0, d[t + 1][tokens:])
                for f in range(t, frames):
                    total = total + jnp.where(local[f] == t, d[f][:tokens], 0.0)
                acc[t, :, cols] = total

    def frame_outputs(i):
        lo, w = groups[i]
        cols = slice(lo, lo + w)
        inside = masks(w)

        def unstacked(x):
            total = x[:tokens]
            for h in range(1, w // head):
                total = jnp.where(inside[h], x[h * tokens : (h + 1) * tokens], total)
            return total.astype(half)

        kcat, vcat = frame_sets(i)
        att = [contract(pst[i][f], vcat[f], 0, 0) for f in each]
        gq = [contract(dst[i][f], kcat[f], 0, 0) for f in each]
        for f in each:
            att_ref[f, :, cols] = unstacked(att[f])
            gq_ref[f, :, cols] = unstacked(gq[f])

    def chip_sum(i):
        when(core == 0, lambda: bwd_near1(i).wait_recv())
        when(core == 1, lambda: bwd_near0(i).wait_recv())
        mine = gouts[i][core].astype(jnp.float32)
        other = gins[i][core].astype(jnp.float32)
        keep_mine = jnp.logical_or(core == 0, mid_outside)
        keep_other = jnp.logical_or(core == 1, mid_outside)
        both = jnp.where(keep_mine, mine, 0.0) + jnp.where(keep_other, other, 0.0)
        gchip_out[i][...] = both.astype(half)
        for k in range(1, reach + 1):
            when(chip >= k, lambda: bwd_chip(i, k).start())
            if i == count - 1:
                when(chip >= k, lambda: bwd_cross(i, k).start())

    def returned(i):
        both = i == count - 1
        for k in range(1, reach + 1):
            when(chip + k < chips, lambda: bwd_chip(i, k).wait_recv())
            if both:
                when(chip + k < chips, lambda: bwd_cross_in(i, k).wait_recv())
        for part in (0, 1) if both else (core,):
            total = None
            for k in range(1, reach + 1):
                term = gchip_in[i][part, k - 1].astype(jnp.float32)
                term = jnp.where(returns[k - 1], term, 0.0)
                total = term if total is None else total + term
            gtots[i][part] = total.astype(half)
        if not both:
            bwd_tot(i).start()

    def finish(i):
        lo, w = groups[i]
        cols = slice(lo, lo + w)
        when(me + 1 < n, lambda: bwd_edge(i).wait_recv())
        if i < count - 1:
            bwd_tot_in(i).wait_recv()
        for part, (acc, result) in enumerate(((acc_k, gk_ref), (acc_v, gv_ref))):
            total = jnp.where(holder, gtots[i][part].astype(jnp.float32), 0.0)
            total = total + jnp.where(mid_in_core0, gins[i][part].astype(jnp.float32), 0.0)
            for t in range(frames):
                value = acc[t, :, cols] + jnp.where(last_open == t, total, 0.0)
                if t == frames - 1:
                    behind = gedge_in[i][part].astype(jnp.float32)
                    value = value + jnp.where(next_prev, behind, 0.0)
                result[t, :, cols] = value.astype(half)

    relay(0)
    for i in range(count):
        fwd_far_in(i).wait_recv()
        when(me > 0, lambda: fwd_edge(i).wait_recv())
        scores(i)
        if i + 1 < count:
            relay(i + 1)
        key_grads(i)
        if i:
            chip_sum(i - 1)
    chip_sum(count - 1)
    frame_outputs(count - 1)
    for i in range(count):
        returned(i)
    for i in range(count):
        finish(i)

    for i in range(count):
        when(core == 0, lambda: fwd_near0(i).wait_send())
        when(core == 1, lambda: fwd_near1(i).wait_send())
        when(core == 0, lambda: bwd_near0(i).wait_send())
        when(core == 1, lambda: bwd_near1(i).wait_send())
        when(me + 1 < n, lambda: fwd_edge(i).wait_send())
        when(me > 0, lambda: bwd_edge(i).wait_send())
        fwd_far(i).wait_send()
        if i < count - 1:
            bwd_tot(i).wait_send()
        for k in range(1, reach + 1):
            when(chip + k < chips, lambda: fwd_chip(i, k).wait_send())
            when(chip >= k, lambda: bwd_chip(i, k).wait_send())
            if i == count - 1:
                when(chip >= k, lambda: bwd_cross(i, k).wait_send())


def store_kernel(*refs):
    count = len(refs) // 2
    sems = refs[-1]
    copies = [
        pltpu.make_async_copy(refs[j], refs[count + j], sems.at[j]) for j in range(count)
    ]
    for copy in copies:
        copy.start()
    for copy in copies:
        copy.wait()


def body(n, queries, keys, values, out_grad, clip_lengths):
    frames, tokens, width = queries.shape
    head = width // HEADS
    reach = min(n // 2 - 1, -(-(MAXCLIP - 1) // (2 * frames)))
    groups = lane_groups(width, head)
    count = len(groups)
    half = jnp.bfloat16
    scratch = [pltpu.SMEM(clip_lengths.shape, jnp.int32)]
    scratch += [pltpu.VMEM((frames, tokens, width), half)] * 2
    scratch += [pltpu.VMEM((frames, tokens, width), jnp.float32)] * 2
    scratch += [pltpu.SemaphoreType.DMA((3 + 2 * count,))]
    scratch += [pltpu.SemaphoreType.DMA((count, 3 + 2 * reach))] * 4
    shapes = [
        lambda w: (2, tokens, w),
        lambda w: (frames + 2, 2, tokens, w),
        lambda w: (tokens, w),
        lambda w: (reach, tokens, w),
        lambda w: (frames, w // head * tokens, w),
        lambda w: (frames, w // head * tokens, w),
        lambda w: (frames, 2 * tokens, w // head * tokens),
        lambda w: (frames, 2 * tokens, w // head * tokens),
        lambda w: (2, tokens, w),
        lambda w: (2, tokens, w),
        lambda w: (tokens, w),
        lambda w: (2, reach, tokens, w),
        lambda w: (2, tokens, w),
        lambda w: (2, tokens, w),
        lambda w: (2, tokens, w),
        lambda w: (2, tokens, w),
    ]
    scratch += [pltpu.VMEM(shape(w), half) for shape in shapes for _, w in groups]
    vmem = pl.BlockSpec(memory_space=pltpu.VMEM)
    hbm = pl.BlockSpec(memory_space=pltpu.HBM)
    like = [jax.ShapeDtypeStruct(queries.shape, half)] * 4
    args = (clip_lengths, queries, keys, values, out_grad)
    results = pl.pallas_call(
        functools.partial(kernel, n, reach, groups, head),
        out_shape=like,
        in_specs=[hbm] * 5,
        out_specs=[vmem] * 4,
        scratch_shapes=scratch,
        compiler_params=pltpu.CompilerParams(
            collective_id=0, has_side_effects=True, vmem_limit_bytes=48 * 1024 * 1024
        ),
    )(*[pltpu.with_memory_space_constraint(a, pltpu.HBM) for a in args])
    return pl.pallas_call(
        store_kernel,
        out_shape=like,
        in_specs=[vmem] * 4,
        out_specs=[hbm] * 4,
        scratch_shapes=[pltpu.SemaphoreType.DMA((4,))],
        compiler_params=pltpu.CompilerParams(vmem_limit_bytes=4 * 1024 * 1024),
    )(*[pltpu.with_memory_space_constraint(a, pltpu.VMEM) for a in results])


def solution(mesh):
    split = P("tm", None, None)
    return jax.shard_map(
        functools.partial(body, mesh.shape["tm"]),
        mesh=mesh,
        in_specs=(split,) * 4 + (P(),),
        out_specs=(split,) * 4,
        check_vma=False,
    )
```

```python
import functools

import jax
import jax.numpy as jnp
from jax import lax
from jax.experimental import pallas as pl
from jax.experimental.pallas import tpu as pltpu
from jax.sharding import PartitionSpec as P

HEADS = 10
MAXCLIP = 24
MESH = pl.DeviceIdType.MESH


def lane_groups(width, head):
    step = max(256, head)
    tiles = [(start, min(step, width - start)) for start in range(0, width, step)]
    groups = []
    for part in (list(enumerate(tiles))[:1], list(enumerate(tiles))[1:]):
        if part:
            lo = part[0][1][0]
            subs = [(j, start - lo, w) for j, (start, w) in part]
            groups.append((lo, sum(w for _, _, w in subs), subs))
    return tiles, groups


def kernel(
    n, reach, tiles, groups, head,
    len_ref, q_ref, k_ref, v_ref, g_ref,
    att_ref, gq_ref, gk_ref, gv_ref,
    lens, q_all, g_all, acc_k, acc_v, lsem, fsend, frecv, bsend, brecv, *bufs,
):
    count = len(groups)
    qst, gst, pst, dst = [bufs[j * len(tiles) : (j + 1) * len(tiles)] for j in range(4)]
    bufs = bufs[4 * len(tiles) :]
    bufs = [bufs[j * count : (j + 1) * count] for j in range(len(bufs) // count)]
    starts, pools, chip_out, chip_in = bufs[:4]
    gouts, gins, gchip_out, gchip_in, gtots, edges, gedge_out, gedge_in = bufs[4:]
    frames, tokens, _ = q_ref.shape
    me = lax.axis_index("tm")
    core = lax.rem(me, 2)
    chip = lax.div(me, 2)
    chips = n // 2
    sibling = me + 1 - 2 * core
    scale = head ** (-0.5)
    near, far = frames, frames + 1
    half = jnp.bfloat16

    loads = [pltpu.make_async_copy(len_ref, lens, lsem.at[0])]
    for i, (lo, w, _) in enumerate(groups):
        for part, ref in enumerate((k_ref, v_ref)):
            loads.append(pltpu.make_async_copy(
                ref.at[:, :, pl.ds(lo, w)], pools[i].at[pl.ds(0, frames), part],
                lsem.at[1 + 2 * i + part],
            ))
    late = [
        pltpu.make_async_copy(q_ref, q_all, lsem.at[1 + 2 * count]),
        pltpu.make_async_copy(g_ref, g_all, lsem.at[2 + 2 * count]),
    ]
    for copy in loads + late:
        copy.start()

    barrier = pltpu.get_barrier_semaphore()

    def greet(device):
        pl.semaphore_signal(barrier, inc=1, device_id=(device,), device_id_type=MESH)

    def ahead(steps):
        return lax.rem(me + steps + n, n)

    greet(ahead(1))
    greet(ahead(-1))
    for k in range(1, reach + 1):
        greet(ahead(2 * k))
        greet(ahead(-2 * k))
    greeted = 2 + 2 * reach

    first = me * frames
    chip_first = chip * (2 * frames)
    wanted = [first + f for f in range(frames)]
    wanted += [chip_first, chip_first + frames, chip_first + 2 * frames - 1]
    wanted += [chip_first + k * 2 * frames for k in range(1, reach + 1)]
    loads[0].wait()

    def scan_clips(c, carry):
        start, owners = carry
        owners = tuple(jnp.where(start <= w, start, o) for w, o in zip(wanted, owners))
        return start + lens[c], owners

    zero = jnp.int32(0)
    _, owners = lax.fori_loop(0, len_ref.shape[0], scan_clips, (zero, (zero,) * len(wanted)))
    own_first, own_mid, own_last = owners[frames : frames + 3]
    own_later = owners[frames + 3 :]
    local = [owners[f] - first for f in range(frames)]
    opening = [local[f] == f for f in range(frames)]
    last_open = jnp.clip(local[frames - 1], 0, frames - 1)
    back = jnp.clip(chip - lax.div(own_first, jnp.int32(2 * frames)), 1, reach)
    away = [
        jnp.where(jnp.logical_and(core == 1, owners[f] >= chip_first), near, far)
        for f in range(frames)
    ]
    owner_slot = [jnp.where(local[f] >= 0, local[f], away[f]) for f in range(frames)]
    prev_slot = [jnp.where(opening[f], f, f - 1) for f in range(1, frames)]
    last_in_core1 = own_last >= chip_first + frames
    mid_outside = own_mid < chip_first
    mid_in_core0 = jnp.logical_and(
        core == 0, jnp.logical_and(own_mid >= chip_first, own_mid < chip_first + frames)
    )
    returns = [
        jnp.logical_and(
            chip + k < chips,
            jnp.logical_and(own_later[k - 1] >= chip_first, own_later[k - 1] < chip_first + 2 * frames),
        )
        for k in range(1, reach + 1)
    ]
    holder = jnp.logical_and(own_last >= first, own_last < first + frames)
    next_first = jnp.where(core == 0, own_mid, own_later[0])
    next_prev = jnp.logical_and(next_first != first + frames, me + 1 < n)

    def ends(src, dst, send_sem, recv_sem, device):
        return pltpu.make_async_remote_copy(
            src_ref=src, dst_ref=dst, send_sem=send_sem, recv_sem=recv_sem,
            device_id=(device,), device_id_type=MESH,
        )

    def remote(src, dst, send, recv, i, slot, device):
        return ends(src, dst, send.at[i, slot], recv.at[i, slot], device)

    fwd_edge = lambda i: remote(
        pools[i].at[frames - 1], edges[i], fsend, frecv, i, 3, ahead(1))
    fwd_near = lambda i: remote(starts[i], pools[i].at[near], fsend, frecv, i, 0, sibling)
    fwd_far = lambda i: remote(
        pools[i].at[far, core], pools[i].at[far, core], fsend, frecv, i, 1, sibling)
    fwd_far_in = lambda i: remote(
        pools[i].at[far, core], pools[i].at[far, 1 - core], fsend, frecv, i, 1, sibling)
    fwd_chip = lambda i, k: remote(
        chip_out[i], chip_in[i].at[k - 1], fsend, frecv, i, 2, ahead(2 * k))
    fwd_chips = lambda i: remote(chip_in[i], chip_in[i], fsend, frecv, i, 2, sibling)
    bwd_edge = lambda i: remote(gedge_out[i], gedge_in[i], bsend, brecv, i, 3, ahead(-1))
    bwd_near = lambda i: remote(gouts[i], gins[i], bsend, brecv, i, 0, sibling)
    bwd_tot = lambda i: remote(
        gtots[i].at[core], gtots[i].at[core], bsend, brecv, i, 1, sibling)
    bwd_tot_in = lambda i: remote(
        gtots[i].at[core], gtots[i].at[1 - core], bsend, brecv, i, 1, sibling)
    bwd_chip = lambda i, k: remote(
        gchip_out[i], gchip_in[i].at[k - 1], bsend, brecv, i, 2, ahead(-2 * k))
    bwd_chips = lambda i: remote(gchip_in[i], gchip_in[i], bsend, brecv, i, 2, sibling)

    for copy in loads[1:]:
        copy.wait()
    for i in range(count):
        start = pools[i][0]
        for f in range(1, frames):
            start = jnp.where(last_open == f, pools[i][f], start)
        starts[i][...] = start
    pl.semaphore_wait(barrier, greeted)

    for i in range(count):
        fwd_near(i).start()
    fwd_edge(0).start()

    for i in range(count):
        fwd_near(i).wait_recv()
        own, other = starts[i][core], pools[i][near, core]
        take_own = jnp.where(core == 1, last_in_core1, jnp.logical_not(last_in_core1))
        chip_out[i][...] = jnp.where(take_own, own, other)
        for k in range(1, reach + 1):
            fwd_chip(i, k).start()
        if i + 1 < count:
            fwd_edge(i + 1).start()

    for copy in late:
        copy.wait()

    def masks(w):
        lane = lax.broadcasted_iota(jnp.int32, (tokens, w), 1)
        return [
            jnp.logical_and(lane >= h * head, lane < (h + 1) * head) for h in range(w // head)
        ]

    for j, (lo, w) in enumerate(tiles):
        keep = [m.astype(jnp.float32).astype(half) for m in masks(w)]
        for f in range(frames):
            for h, m in enumerate(keep):
                rows = slice(h * tokens, (h + 1) * tokens)
                qst[j][f, rows] = q_all[f, :, lo : lo + w] * m
                gst[j][f, rows] = g_all[f, :, lo : lo + w] * m

    def contract(a, b, ca, cb):
        return lax.dot_general(
            a, b, (((ca,), (cb,)), ((), ())), preferred_element_type=jnp.float32
        )

    def relay(i):
        fwd_chips(i).wait_recv()
        pools[i][far, core] = chip_in[i][back - 1]
        fwd_far(i).start()

    each = range(frames)

    def frame_sets(i):
        own = [pools[i][owner_slot[f]] for f in each]
        prev = [jnp.where(opening[0], pools[i][0], edges[i][...])]
        prev += [pools[i][prev_slot[f - 1]] for f in each[1:]]
        return [
            [jnp.concatenate([own[f][part], prev[f][part]], axis=0) for f in each]
            for part in range(2)
        ]

    def scores(i):
        kcat, vcat = frame_sets(i)
        pairs = [(f, j, slice(off, off + w)) for j, off, w in groups[i][2] for f in each]
        s = [contract(kcat[f][:, c], qst[j][f], 1, 1) * scale for f, j, c in pairs]
        dp = [contract(vcat[f][:, c], gst[j][f], 1, 1) for f, j, c in pairs]
        if i:
            frame_outputs(i - 1)
        e = [jnp.exp(x - jnp.max(x, axis=0, keepdims=True)) for x in s]
        p = [x * (1.0 / jnp.sum(x, axis=0, keepdims=True)) for x in e]
        for (f, j, _), x, d in zip(pairs, p, dp):
            pst[j][f] = x.astype(half)
            dst[j][f] = (x * (d - jnp.sum(x * d, axis=0, keepdims=True)) * scale).astype(half)

    def key_grads(i):
        lo = groups[i][0]
        for j, off, w in groups[i][2]:
            here, cols = slice(off, off + w), slice(lo + off, lo + off + w)
            dk = [contract(dst[j][f], qst[j][f], 1, 0) for f in each]
            dv = [contract(pst[j][f], gst[j][f], 1, 0) for f in each]
            for part, (d, acc) in enumerate(((dk, acc_k), (dv, acc_v))):
                gedge_out[i][part, :, here] = d[0][tokens:].astype(half)
                out = jnp.zeros((tokens, w), jnp.float32)
                for f in each:
                    out = out + jnp.where(local[f] < 0, d[f][:tokens], 0.0)
                gouts[i][part, :, here] = out.astype(half)
                for t in each:
                    total = jnp.where(opening[t], d[t][tokens:], 0.0)
                    if t + 1 < frames:
                        total = total + jnp.where(opening[t + 1], 0.0, d[t + 1][tokens:])
                    for f in range(t, frames):
                        total = total + jnp.where(local[f] == t, d[f][:tokens], 0.0)
                    acc[t, :, cols] = total
        bwd_near(i).start()
        bwd_edge(i).start()

    def frame_outputs(i):
        lo = groups[i][0]
        kcat, vcat = frame_sets(i)
        for j, off, w in groups[i][2]:
            here, cols = slice(off, off + w), slice(lo + off, lo + off + w)
            inside = masks(w)

            def unstacked(x):
                total = x[:tokens]
                for h in range(1, w // head):
                    total = jnp.where(inside[h], x[h * tokens : (h + 1) * tokens], total)
                return total.astype(half)

            att = [contract(pst[j][f], vcat[f][:, here], 0, 0) for f in each]
            gq = [contract(dst[j][f], kcat[f][:, here], 0, 0) for f in each]
            for f in each:
                att_ref[f, :, cols] = unstacked(att[f])
                gq_ref[f, :, cols] = unstacked(gq[f])

    def chip_sum(i):
        bwd_near(i).wait_recv()
        mine = gouts[i][core].astype(jnp.float32)
        other = gins[i][core].astype(jnp.float32)
        keep_mine = jnp.logical_or(core == 0, mid_outside)
        keep_other = jnp.logical_or(core == 1, mid_outside)
        both = jnp.where(keep_mine, mine, 0.0) + jnp.where(keep_other, other, 0.0)
        gchip_out[i][...] = both.astype(half)
        for k in range(1, reach + 1):
            bwd_chip(i, k).start()

    def returned(i):
        bwd_chips(i).wait_recv()
        total = None
        for k in range(1, reach + 1):
            term = jnp.where(returns[k - 1], gchip_in[i][k - 1].astype(jnp.float32), 0.0)
            total = term if total is None else total + term
        gtots[i][core] = total.astype(half)
        bwd_tot(i).start()

    def finish(i):
        lo, w, _ = groups[i]
        cols = slice(lo, lo + w)
        bwd_edge(i).wait_recv()
        bwd_tot_in(i).wait_recv()
        for part, (acc, result) in enumerate(((acc_k, gk_ref), (acc_v, gv_ref))):
            total = jnp.where(holder, gtots[i][part].astype(jnp.float32), 0.0)
            total = total + jnp.where(mid_in_core0, gins[i][part].astype(jnp.float32), 0.0)
            for t in range(frames):
                value = acc[t, :, cols] + jnp.where(last_open == t, total, 0.0)
                if t == frames - 1:
                    behind = gedge_in[i][part].astype(jnp.float32)
                    value = value + jnp.where(next_prev, behind, 0.0)
                result[t, :, cols] = value.astype(half)

    relay(0)
    for i in range(count):
        fwd_far_in(i).wait_recv()
        fwd_edge(i).wait_recv()
        scores(i)
        if i + 1 < count:
            relay(i + 1)
        key_grads(i)
        if i:
            chip_sum(i - 1)
    chip_sum(count - 1)
    frame_outputs(count - 1)
    for i in range(count):
        returned(i)
    for i in range(count):
        finish(i)

    for i in range(count):
        for copy in (fwd_near, fwd_edge, fwd_far, fwd_chips, bwd_near, bwd_edge, bwd_tot, bwd_chips):
            copy(i).wait_send()


def store_kernel(*refs):
    count = len(refs) // 2
    sems = refs[-1]
    copies = [
        pltpu.make_async_copy(refs[j], refs[count + j], sems.at[j]) for j in range(count)
    ]
    for copy in copies:
        copy.start()
    for copy in copies:
        copy.wait()


def body(n, queries, keys, values, out_grad, clip_lengths):
    frames, tokens, width = queries.shape
    head = width // HEADS
    reach = min(n // 2 - 1, -(-(MAXCLIP - 1) // (2 * frames)))
    tiles, groups = lane_groups(width, head)
    count = len(groups)
    half = jnp.bfloat16
    scratch = [pltpu.SMEM(clip_lengths.shape, jnp.int32)]
    scratch += [pltpu.VMEM((frames, tokens, width), half)] * 2
    scratch += [pltpu.VMEM((frames, tokens, width), jnp.float32)] * 2
    scratch += [pltpu.SemaphoreType.DMA((3 + 2 * count,))]
    scratch += [pltpu.SemaphoreType.DMA((count, 4))] * 4
    stacked = [pltpu.VMEM((frames, w // head * tokens, w), half) for _, w in tiles]
    probs = [pltpu.VMEM((frames, 2 * tokens, w // head * tokens), half) for _, w in tiles]
    scratch += stacked * 2 + probs * 2
    shapes = [
        lambda w: (2, tokens, w),
        lambda w: (frames + 2, 2, tokens, w),
        lambda w: (tokens, w),
        lambda w: (reach, tokens, w),
        lambda w: (2, tokens, w),
        lambda w: (2, tokens, w),
        lambda w: (tokens, w),
        lambda w: (reach, tokens, w),
        lambda w: (2, tokens, w),
        lambda w: (2, tokens, w),
        lambda w: (2, tokens, w),
        lambda w: (2, tokens, w),
    ]
    scratch += [pltpu.VMEM(shape(w), half) for shape in shapes for _, w, _ in groups]
    vmem = pl.BlockSpec(memory_space=pltpu.VMEM)
    hbm = pl.BlockSpec(memory_space=pltpu.HBM)
    like = [jax.ShapeDtypeStruct(queries.shape, half)] * 4
    args = (clip_lengths, queries, keys, values, out_grad)
    results = pl.pallas_call(
        functools.partial(kernel, n, reach, tiles, groups, head),
        out_shape=like,
        in_specs=[hbm] * 5,
        out_specs=[vmem] * 4,
        scratch_shapes=scratch,
        compiler_params=pltpu.CompilerParams(
            collective_id=0, has_side_effects=True, vmem_limit_bytes=48 * 1024 * 1024
        ),
    )(*[pltpu.with_memory_space_constraint(a, pltpu.HBM) for a in args])
    return pl.pallas_call(
        store_kernel,
        out_shape=like,
        in_specs=[vmem] * 4,
        out_specs=[hbm] * 4,
        scratch_shapes=[pltpu.SemaphoreType.DMA((4,))],
        compiler_params=pltpu.CompilerParams(vmem_limit_bytes=4 * 1024 * 1024),
    )(*[pltpu.with_memory_space_constraint(a, pltpu.VMEM) for a in results])


def solution(mesh):
    split = P("tm", None, None)
    return jax.shard_map(
        functools.partial(body, mesh.shape["tm"]),
        mesh=mesh,
        in_specs=(split,) * 4 + (P(),),
        out_specs=(split,) * 4,
        check_vma=False,
    )
```

```python
import functools

import jax
import jax.numpy as jnp
from jax import lax
from jax.experimental import pallas as pl
from jax.experimental.pallas import tpu as pltpu
from jax.sharding import PartitionSpec as P

HEADS = 10
MAXCLIP = 24
MESH = pl.DeviceIdType.MESH


def lane_groups(width, head):
    step = max(256, head)
    tiles = [(start, min(step, width - start)) for start in range(0, width, step)]
    groups = []
    for part in (list(enumerate(tiles))[:1], list(enumerate(tiles))[1:]):
        if part:
            lo = part[0][1][0]
            subs = [(j, start - lo, w) for j, (start, w) in part]
            groups.append((lo, sum(w for _, _, w in subs), subs))
    return tiles, groups


def kernel(
    n, reach, tiles, groups, head,
    len_ref, q_ref, k_ref, v_ref, g_ref,
    att_ref, gq_ref, gk_ref, gv_ref,
    lens, q_all, g_all, acc_k, acc_v, lsem, fsend, frecv, bsend, brecv, *bufs,
):
    count = len(groups)
    qst, gst, pst, dst = [bufs[j * len(tiles) : (j + 1) * len(tiles)] for j in range(4)]
    bufs = bufs[4 * len(tiles) :]
    bufs = [bufs[j * count : (j + 1) * count] for j in range(len(bufs) // count)]
    starts, pools, chip_out, chip_in = bufs[:4]
    gouts, gins, gchip_out, gchip_in, gtots, edges, gedge_out, gedge_in = bufs[4:]
    frames, tokens, _ = q_ref.shape
    me = lax.axis_index("tm")
    core = lax.rem(me, 2)
    chip = lax.div(me, 2)
    chips = n // 2
    sibling = me + 1 - 2 * core
    scale = head ** (-0.5)
    near, far = frames, frames + 1
    half = jnp.bfloat16

    loads = [pltpu.make_async_copy(len_ref, lens, lsem.at[0])]
    for i, (lo, w, _) in enumerate(groups):
        for part, ref in enumerate((k_ref, v_ref)):
            loads.append(pltpu.make_async_copy(
                ref.at[:, :, pl.ds(lo, w)], pools[i].at[pl.ds(0, frames), part],
                lsem.at[1 + 2 * i + part],
            ))
    late = [
        pltpu.make_async_copy(q_ref, q_all, lsem.at[1 + 2 * count]),
        pltpu.make_async_copy(g_ref, g_all, lsem.at[2 + 2 * count]),
    ]
    for copy in loads + late:
        copy.start()

    barrier = pltpu.get_barrier_semaphore()

    def greet(device):
        pl.semaphore_signal(barrier, inc=1, device_id=(device,), device_id_type=MESH)

    def ahead(steps):
        return lax.rem(me + steps + n, n)

    def when(condition, act):
        @pl.when(condition)
        def _():
            act()

    when(me + 1 < n, lambda: greet(ahead(1)))
    when(me > 0, lambda: greet(ahead(-1)))
    for k in range(1, reach + 1):
        when(chip + k < chips, lambda: greet(ahead(2 * k)))
        when(chip >= k, lambda: greet(ahead(-2 * k)))
    greeted = jnp.minimum(1, me) + jnp.minimum(1, n - 1 - me)
    greeted += jnp.minimum(reach, chips - 1 - chip) + jnp.minimum(reach, chip)

    first = me * frames
    chip_first = chip * (2 * frames)
    wanted = [first + f for f in range(frames)]
    wanted += [chip_first, chip_first + frames, chip_first + 2 * frames - 1]
    wanted += [chip_first + k * 2 * frames for k in range(1, reach + 1)]
    loads[0].wait()

    def scan_clips(c, carry):
        start, owners = carry
        owners = tuple(jnp.where(start <= w, start, o) for w, o in zip(wanted, owners))
        return start + lens[c], owners

    zero = jnp.int32(0)
    _, owners = lax.fori_loop(0, len_ref.shape[0], scan_clips, (zero, (zero,) * len(wanted)))
    own_first, own_mid, own_last = owners[frames : frames + 3]
    own_later = owners[frames + 3 :]
    local = [owners[f] - first for f in range(frames)]
    opening = [local[f] == f for f in range(frames)]
    last_open = jnp.clip(local[frames - 1], 0, frames - 1)
    back = jnp.clip(chip - lax.div(own_first, jnp.int32(2 * frames)), 1, reach)
    away = [
        jnp.where(jnp.logical_and(core == 1, owners[f] >= chip_first), near, far)
        for f in range(frames)
    ]
    owner_slot = [jnp.where(local[f] >= 0, local[f], away[f]) for f in range(frames)]
    prev_slot = [jnp.where(opening[f], f, f - 1) for f in range(1, frames)]
    last_in_core1 = own_last >= chip_first + frames
    mid_outside = own_mid < chip_first
    mid_in_core0 = jnp.logical_and(
        core == 0, jnp.logical_and(own_mid >= chip_first, own_mid < chip_first + frames)
    )
    returns = [
        jnp.logical_and(
            chip + k < chips,
            jnp.logical_and(own_later[k - 1] >= chip_first, own_later[k - 1] < chip_first + 2 * frames),
        )
        for k in range(1, reach + 1)
    ]
    holder = jnp.logical_and(own_last >= first, own_last < first + frames)
    next_first = jnp.where(core == 0, own_mid, own_later[0])
    next_prev = jnp.logical_and(next_first != first + frames, me + 1 < n)

    def ends(src, dst, send_sem, recv_sem, device):
        return pltpu.make_async_remote_copy(
            src_ref=src, dst_ref=dst, send_sem=send_sem, recv_sem=recv_sem,
            device_id=(device,), device_id_type=MESH,
        )

    def remote(src, dst, send, recv, i, slot, device):
        return ends(src, dst, send.at[i, slot], recv.at[i, slot], device)

    fwd_edge = lambda i: remote(
        pools[i].at[frames - 1], edges[i], fsend, frecv, i, 2, ahead(1))
    fwd_near = lambda i: remote(starts[i], pools[i].at[near], fsend, frecv, i, 0, sibling)
    fwd_far = lambda i: remote(
        pools[i].at[far, core], pools[i].at[far, core], fsend, frecv, i, 1, sibling)
    fwd_far_in = lambda i: remote(
        pools[i].at[far, core], pools[i].at[far, 1 - core], fsend, frecv, i, 1, sibling)
    fwd_chip = lambda i, k: remote(
        chip_out[i], chip_in[i].at[k - 1], fsend, frecv, i, 3 + k, ahead(2 * k))
    bwd_edge = lambda i: remote(gedge_out[i], gedge_in[i], bsend, brecv, i, 2, ahead(-1))
    bwd_near = lambda i: remote(gouts[i], gins[i], bsend, brecv, i, 0, sibling)
    bwd_tot = lambda i: remote(
        gtots[i].at[core], gtots[i].at[core], bsend, brecv, i, 1, sibling)
    bwd_tot_in = lambda i: remote(
        gtots[i].at[core], gtots[i].at[1 - core], bsend, brecv, i, 1, sibling)
    bwd_chip = lambda i, k: remote(
        gchip_out[i], gchip_in[i].at[k - 1], bsend, brecv, i, 3 + k, ahead(-2 * k))

    for copy in loads[1:]:
        copy.wait()
    for i in range(count):
        start = pools[i][0]
        for f in range(1, frames):
            start = jnp.where(last_open == f, pools[i][f], start)
        starts[i][...] = start
    pl.semaphore_wait(barrier, greeted)

    for i in range(count):
        fwd_near(i).start()
    when(me + 1 < n, lambda: fwd_edge(0).start())

    for i in range(count):
        fwd_near(i).wait_recv()
        own, other = starts[i][core], pools[i][near, core]
        take_own = jnp.where(core == 1, last_in_core1, jnp.logical_not(last_in_core1))
        chip_out[i][...] = jnp.where(take_own, own, other)
        for k in range(1, reach + 1):
            when(chip + k < chips, lambda: fwd_chip(i, k).start())
        if i + 1 < count:
            when(me + 1 < n, lambda: fwd_edge(i + 1).start())

    for copy in late:
        copy.wait()

    def masks(w):
        lane = lax.broadcasted_iota(jnp.int32, (tokens, w), 1)
        return [
            jnp.logical_and(lane >= h * head, lane < (h + 1) * head) for h in range(w // head)
        ]

    for j, (lo, w) in enumerate(tiles):
        keep = [m.astype(jnp.float32).astype(half) for m in masks(w)]
        for f in range(frames):
            for h, m in enumerate(keep):
                rows = slice(h * tokens, (h + 1) * tokens)
                qst[j][f, rows] = q_all[f, :, lo : lo + w] * m
                gst[j][f, rows] = g_all[f, :, lo : lo + w] * m

    def contract(a, b, ca, cb):
        return lax.dot_general(
            a, b, (((ca,), (cb,)), ((), ())), preferred_element_type=jnp.float32
        )

    def relay(i):
        for k in range(1, reach + 1):
            when(chip >= k, lambda: fwd_chip(i, k).wait_recv())
        pools[i][far, core] = chip_in[i][back - 1]
        fwd_far(i).start()

    each = range(frames)

    def frame_sets(i):
        own = [pools[i][owner_slot[f]] for f in each]
        prev = [jnp.where(opening[0], pools[i][0], edges[i][...])]
        prev += [pools[i][prev_slot[f - 1]] for f in each[1:]]
        return [
            [jnp.concatenate([own[f][part], prev[f][part]], axis=0) for f in each]
            for part in range(2)
        ]

    def scores(i):
        kcat, vcat = frame_sets(i)
        pairs = [(f, j, slice(off, off + w)) for j, off, w in groups[i][2] for f in each]
        s = [contract(kcat[f][:, c], qst[j][f], 1, 1) * scale for f, j, c in pairs]
        dp = [contract(vcat[f][:, c], gst[j][f], 1, 1) for f, j, c in pairs]
        if i:
            frame_outputs(i - 1)
        e = [jnp.exp(x - jnp.max(x, axis=0, keepdims=True)) for x in s]
        p = [x * (1.0 / jnp.sum(x, axis=0, keepdims=True)) for x in e]
        for (f, j, _), x, d in zip(pairs, p, dp):
            pst[j][f] = x.astype(half)
            dst[j][f] = (x * (d - jnp.sum(x * d, axis=0, keepdims=True)) * scale).astype(half)

    def key_grads(i):
        lo = groups[i][0]
        for j, off, w in groups[i][2]:
            here, cols = slice(off, off + w), slice(lo + off, lo + off + w)
            dk = [contract(dst[j][f], qst[j][f], 1, 0) for f in each]
            dv = [contract(pst[j][f], gst[j][f], 1, 0) for f in each]
            for part, (d, acc) in enumerate(((dk, acc_k), (dv, acc_v))):
                gedge_out[i][part, :, here] = d[0][tokens:].astype(half)
                out = jnp.zeros((tokens, w), jnp.float32)
                for f in each:
                    out = out + jnp.where(local[f] < 0, d[f][:tokens], 0.0)
                gouts[i][part, :, here] = out.astype(half)
                for t in each:
                    total = jnp.where(opening[t], d[t][tokens:], 0.0)
                    if t + 1 < frames:
                        total = total + jnp.where(opening[t + 1], 0.0, d[t + 1][tokens:])
                    for f in range(t, frames):
                        total = total + jnp.where(local[f] == t, d[f][:tokens], 0.0)
                    acc[t, :, cols] = total
        bwd_near(i).start()
        when(me > 0, lambda: bwd_edge(i).start())

    def frame_outputs(i):
        lo = groups[i][0]
        kcat, vcat = frame_sets(i)
        for j, off, w in groups[i][2]:
            here, cols = slice(off, off + w), slice(lo + off, lo + off + w)
            inside = masks(w)

            def unstacked(x):
                total = x[:tokens]
                for h in range(1, w // head):
                    total = jnp.where(inside[h], x[h * tokens : (h + 1) * tokens], total)
                return total.astype(half)

            att = [contract(pst[j][f], vcat[f][:, here], 0, 0) for f in each]
            gq = [contract(dst[j][f], kcat[f][:, here], 0, 0) for f in each]
            for f in each:
                att_ref[f, :, cols] = unstacked(att[f])
                gq_ref[f, :, cols] = unstacked(gq[f])

    def chip_sum(i):
        bwd_near(i).wait_recv()
        mine = gouts[i][core].astype(jnp.float32)
        other = gins[i][core].astype(jnp.float32)
        keep_mine = jnp.logical_or(core == 0, mid_outside)
        keep_other = jnp.logical_or(core == 1, mid_outside)
        both = jnp.where(keep_mine, mine, 0.0) + jnp.where(keep_other, other, 0.0)
        gchip_out[i][...] = both.astype(half)
        for k in range(1, reach + 1):
            when(chip >= k, lambda: bwd_chip(i, k).start())

    def returned(i):
        for k in range(1, reach + 1):
            when(chip + k < chips, lambda: bwd_chip(i, k).wait_recv())
        total = None
        for k in range(1, reach + 1):
            term = jnp.where(returns[k - 1], gchip_in[i][k - 1].astype(jnp.float32), 0.0)
            total = term if total is None else total + term
        gtots[i][core] = total.astype(half)
        bwd_tot(i).start()

    def finish(i):
        lo, w, _ = groups[i]
        cols = slice(lo, lo + w)
        when(me + 1 < n, lambda: bwd_edge(i).wait_recv())
        bwd_tot_in(i).wait_recv()
        for part, (acc, result) in enumerate(((acc_k, gk_ref), (acc_v, gv_ref))):
            total = jnp.where(holder, gtots[i][part].astype(jnp.float32), 0.0)
            total = total + jnp.where(mid_in_core0, gins[i][part].astype(jnp.float32), 0.0)
            for t in range(frames):
                value = acc[t, :, cols] + jnp.where(last_open == t, total, 0.0)
                if t == frames - 1:
                    behind = gedge_in[i][part].astype(jnp.float32)
                    value = value + jnp.where(next_prev, behind, 0.0)
                result[t, :, cols] = value.astype(half)

    relay(0)
    for i in range(count):
        fwd_far_in(i).wait_recv()
        when(me > 0, lambda: fwd_edge(i).wait_recv())
        scores(i)
        if i + 1 < count:
            relay(i + 1)
        key_grads(i)
        if i:
            chip_sum(i - 1)
    chip_sum(count - 1)
    frame_outputs(count - 1)
    for i in range(count):
        returned(i)
    for i in range(count):
        finish(i)

    for i in range(count):
        for copy in (fwd_near, fwd_far, bwd_near, bwd_tot):
            copy(i).wait_send()
        when(me + 1 < n, lambda: fwd_edge(i).wait_send())
        when(me > 0, lambda: bwd_edge(i).wait_send())
        for k in range(1, reach + 1):
            when(chip + k < chips, lambda: fwd_chip(i, k).wait_send())
            when(chip >= k, lambda: bwd_chip(i, k).wait_send())


def store_kernel(*refs):
    count = len(refs) // 2
    sems = refs[-1]
    copies = [
        pltpu.make_async_copy(refs[j], refs[count + j], sems.at[j]) for j in range(count)
    ]
    for copy in copies:
        copy.start()
    for copy in copies:
        copy.wait()


def body(n, queries, keys, values, out_grad, clip_lengths):
    frames, tokens, width = queries.shape
    head = width // HEADS
    reach = min(n // 2 - 1, -(-(MAXCLIP - 1) // (2 * frames)))
    tiles, groups = lane_groups(width, head)
    count = len(groups)
    half = jnp.bfloat16
    scratch = [pltpu.SMEM(clip_lengths.shape, jnp.int32)]
    scratch += [pltpu.VMEM((frames, tokens, width), half)] * 2
    scratch += [pltpu.VMEM((frames, tokens, width), jnp.float32)] * 2
    scratch += [pltpu.SemaphoreType.DMA((3 + 2 * count,))]
    scratch += [pltpu.SemaphoreType.DMA((count, 4 + reach))] * 4
    stacked = [pltpu.VMEM((frames, w // head * tokens, w), half) for _, w in tiles]
    probs = [pltpu.VMEM((frames, 2 * tokens, w // head * tokens), half) for _, w in tiles]
    scratch += stacked * 2 + probs * 2
    shapes = [
        lambda w: (2, tokens, w),
        lambda w: (frames + 2, 2, tokens, w),
        lambda w: (tokens, w),
        lambda w: (reach, tokens, w),
        lambda w: (2, tokens, w),
        lambda w: (2, tokens, w),
        lambda w: (tokens, w),
        lambda w: (reach, tokens, w),
        lambda w: (2, tokens, w),
        lambda w: (2, tokens, w),
        lambda w: (2, tokens, w),
        lambda w: (2, tokens, w),
    ]
    scratch += [pltpu.VMEM(shape(w), half) for shape in shapes for _, w, _ in groups]
    vmem = pl.BlockSpec(memory_space=pltpu.VMEM)
    hbm = pl.BlockSpec(memory_space=pltpu.HBM)
    like = [jax.ShapeDtypeStruct(queries.shape, half)] * 4
    args = (clip_lengths, queries, keys, values, out_grad)
    results = pl.pallas_call(
        functools.partial(kernel, n, reach, tiles, groups, head),
        out_shape=like,
        in_specs=[hbm] * 5,
        out_specs=[vmem] * 4,
        scratch_shapes=scratch,
        compiler_params=pltpu.CompilerParams(
            collective_id=0, has_side_effects=True, vmem_limit_bytes=48 * 1024 * 1024
        ),
    )(*[pltpu.with_memory_space_constraint(a, pltpu.HBM) for a in args])
    return pl.pallas_call(
        store_kernel,
        out_shape=like,
        in_specs=[vmem] * 4,
        out_specs=[hbm] * 4,
        scratch_shapes=[pltpu.SemaphoreType.DMA((4,))],
        compiler_params=pltpu.CompilerParams(vmem_limit_bytes=4 * 1024 * 1024),
    )(*[pltpu.with_memory_space_constraint(a, pltpu.VMEM) for a in results])


def solution(mesh):
    split = P("tm", None, None)
    return jax.shard_map(
        functools.partial(body, mesh.shape["tm"]),
        mesh=mesh,
        in_specs=(split,) * 4 + (P(),),
        out_specs=(split,) * 4,
        check_vma=False,
    )
```
